256 devices in a mesh: dp: 16 (over x, y_lo, core), mp: 16 (over y_hi, z).
Axes of the slice: x: 4, y: 4 (y_hi: 2, y_lo: 2; y = y_hi * 2 + y_lo), z: 8, core: 2. Of those that a mesh axis runs over, the one named last changes fastest.
Arguments:
- tokens: bfloat16 [4096, 6144], P('dp', 'mp'), may hold values from -36 to 36
- w_qkv: bfloat16 [6144, 12288], P('dp', 'mp'), may hold values from -0.078125 to 0.078125
- out_grad: bfloat16 [4096, 4096], P('dp', 'mp'), may hold values from -24 to 24
Outputs:
- attended: bfloat16 [4096, 4096], P('dp', 'mp')
- grad_tokens: float32 [4096, 6144], P('dp', 'mp')
- grad_qkv: bfloat16 [6144, 12288], P('dp', 'mp')
The draws below stay inside these ranges and needn't reach their ends.
All inputs are finite; a program needn't handle non-finite values.
Results may differ from the reference program's by a relative error of at most 0.023.
Values may be sent and summed in bfloat16 or wider, within the bound.
A program may use at most 128 MiB of HBM per device.

```python
import jax
import jax.numpy as jnp
from jax import lax

D = 6144
HD = 128
SEQ = 256
TOK_DEV = 256
TOKENS = 4096
HEADS = 32
QKV_DEV = 768


def draw_tokens(key, part):
    key = jax.random.fold_in(key, 11)
    first, second, third = jax.random.split(key, 3)
    row_scale = jnp.exp(jax.random.uniform(second, (TOKENS, 1), jnp.float32, jnp.log(0.3), jnp.log(3.0)))
    col_scale = jnp.exp(jax.random.uniform(third, (1, D), jnp.float32, jnp.log(0.3), jnp.log(3.0)))
    base = jax.random.normal(first, (TOKENS, D), jnp.float32)
    base = jnp.clip(base, -4.0, 4.0)
    return (base * row_scale * col_scale).astype(jnp.bfloat16)


def block_levels(stream_key, shape, shards, least, largest):
    loudness, own = 1.0, jax.random.fold_in(stream_key, 6)
    for position, parts in shards:
        steps = jnp.exp(jax.random.uniform(jax.random.fold_in(own, position), (parts,), jnp.float32, least / len(shards), largest / len(shards)))
        loudness = loudness * jnp.repeat(steps, shape[position] // parts).reshape([-1 if axis == position else 1 for axis in range(len(shape))])
    return loudness


def gaussian(stream_key, dims, spread, most, pieces=(), kind=jnp.bfloat16):
    loudness = block_levels(stream_key, dims, pieces, -0.22, 0.18) if pieces else 1.0
    values = jax.random.normal(stream_key, dims, jnp.float32) * spread * loudness
    return jnp.minimum(jnp.maximum(values, -most), most).astype(kind)


def setup_inputs(seed: int = 0) -> dict:
    seeds = jax.random.split(jax.random.key(seed), 4)
    return {
        "tokens": draw_tokens(jax.random.fold_in(seeds[3], 71), 0),
        "w_qkv": gaussian(seeds[1], (D, 3 * HEADS * HD), D ** -0.5, 0.078125, ((0, 16), (1, 16))),
        "out_grad": gaussian(seeds[2], (TOKENS, HEADS * HD), 4.0, 24.0, ((0, 16), (1, 16))),
    }


def normalize_rows(values_in):
    as_float = values_in.astype(jnp.float32)
    centred = as_float - lax.optimization_barrier(jnp.mean(as_float, axis=-1, keepdims=True))
    inv_scale = lax.rsqrt(lax.optimization_barrier(jnp.mean(centred * centred, axis=-1, keepdims=True)) + 1e-06)
    return (centred * inv_scale, inv_scale)

def attention(packed):
    head_count = packed.shape[1] // (3 * HD)
    shaped = packed.reshape(-1, SEQ, head_count, 3, HD)
    query_unit, _ = normalize_rows(shaped[:, :, :, 0, :])
    key_unit, _ = normalize_rows(shaped[:, :, :, 1, :])
    value_rows = shaped[:, :, :, 2, :]
    scores = jnp.einsum('bqhd,bkhd->bhqk', query_unit, key_unit, precision=lax.Precision.HIGHEST) / jnp.sqrt(jnp.float32(HD))
    weights = jnp.exp(scores)
    probs = weights / lax.optimization_barrier(jnp.sum(weights, axis=-1, keepdims=True))
    result = jnp.einsum('bhqk,bkhd->bqhd', probs, value_rows, precision=lax.Precision.HIGHEST)
    return result.reshape(packed.shape[0], head_count * HD)

def reference(tokens, w_qkv, out_grad):
    unit, inv_scale = normalize_rows(tokens)
    normed = unit.astype(jnp.bfloat16)
    qkv = jnp.dot(normed, w_qkv, preferred_element_type=jnp.float32).astype(jnp.bfloat16)
    attended, pullback = jax.vjp(attention, qkv.astype(jnp.float32))
    d_qkv = pullback(out_grad.astype(jnp.float32))[0].astype(jnp.bfloat16)
    width = w_qkv.shape[1]
    token_blocks = normed.reshape(TOKENS // TOK_DEV, TOK_DEV, D)
    grad_blocks = d_qkv.reshape(TOKENS // TOK_DEV, TOK_DEV, width)

    def add_group(total, pair):
        term = lax.dot_general(pair[0], pair[1], (((0,), (0,)), ((), ())), preferred_element_type=jnp.float32)
        rounded = lax.optimization_barrier(term.astype(jnp.bfloat16))
        return (total + rounded.astype(jnp.float32), 0)
    grad_total, _ = lax.scan(add_group, jnp.zeros((D, width), jnp.float32), (token_blocks, grad_blocks))
    column_count = width // QKV_DEV
    grad_cols = d_qkv.reshape(TOKENS, column_count, QKV_DEV).transpose(1, 0, 2)
    weight_cols = w_qkv.reshape(D, column_count, QKV_DEV).transpose(1, 0, 2)

    def add_heads(total, pair):
        term = lax.dot_general(pair[0], pair[1], (((1,), (1,)), ((), ())), preferred_element_type=jnp.float32)
        rounded = lax.optimization_barrier(term.astype(jnp.bfloat16))
        return (total + rounded.astype(jnp.float32), 0)
    d_normed, _ = lax.scan(add_heads, jnp.zeros((TOKENS, D), jnp.float32), (grad_cols, weight_cols))
    grad_tokens = inv_scale * (d_normed - lax.optimization_barrier(jnp.mean(d_normed, axis=-1, keepdims=True)) - unit * lax.optimization_barrier(jnp.mean(d_normed * unit, axis=-1, keepdims=True)))
    return (attended.astype(jnp.bfloat16), grad_tokens, grad_total.astype(jnp.bfloat16))
```

```python
import jax
import jax.numpy as jnp
from jax import lax
from jax.experimental import pallas as pl
from jax.experimental.pallas import tpu as pltpu
from jax.sharding import PartitionSpec as P

HD = 128
EPS = 1e-06
F32 = jnp.float32
BF16 = jnp.bfloat16
MESH = pl.DeviceIdType.MESH


def mm(a, b, dims, precision=None):
    return lax.dot_general(
        a, b, (dims, ((), ())), preferred_element_type=F32, precision=precision
    )


def normalize(v):
    centred = v - jnp.mean(v, axis=-1, keepdims=True)
    inv = lax.rsqrt(jnp.mean(centred * centred, axis=-1, keepdims=True) + EPS)
    return centred * inv, inv


def normalize_back(d, unit, inv):
    return inv * (
        d
        - jnp.mean(d, axis=-1, keepdims=True)
        - unit * jnp.mean(d * unit, axis=-1, keepdims=True)
    )


def one_head(q, k, v, og):
    qu, qi = normalize(q.astype(F32))
    ku, ki = normalize(k.astype(F32))
    scale = 1.0 / (HD**0.5)
    scores = mm(qu, ku, ((1,), (1,)), lax.Precision.HIGHEST) * scale
    weights = jnp.exp(scores)
    probs = weights / jnp.sum(weights, axis=-1, keepdims=True)
    probs16 = probs.astype(BF16)
    out = mm(probs16, v, ((1,), (0,)))
    dv = mm(probs16, og, ((0,), (0,)))
    dp = mm(og, v, ((1,), (1,)))
    ds = (probs * (dp - jnp.sum(dp * probs, axis=-1, keepdims=True)) * scale).astype(BF16)
    dq = normalize_back(mm(ds, ku.astype(BF16), ((1,), (0,))), qu, qi)
    dk = normalize_back(mm(ds, qu.astype(BF16), ((0,), (0,))), ku, ki)
    return out, dq, dk, dv


def kernel(
    tok_ref, w_ref, og_ref,
    att_ref, gt_ref, gw_ref,
    wfull, tfull, normed, normt, acc, qkv, dqkv,
    gown, gout, gin, gya, gxq, gxh, gyb,
    bk, bh, bw, by, stat_out, stat_in,
    send_sem, recv_sem, stat_send, stat_recv,
):
    dp, mp = lax.axis_index("dp"), lax.axis_index("mp")
    x, y, c = dp // 4, (dp // 2) % 2, dp % 2
    yh, z = mp // 8, mp % 8
    rows, width = tok_ref.shape
    depth = w_ref.shape[0]
    half, quarter = depth // 2, depth // 4
    hrow = rows // 2

    def ring(v, d, n):
        return lax.rem(v + d + n, n)

    sib = {"dp": dp + 1 - 2 * c}
    ydev = {"dp": x * 4 + (1 - y) * 2 + c}
    xdev = {d: {"dp": ring(x, d, 4) * 4 + y * 2 + c} for d in (1, -1)}
    zdev = {d: {"mp": yh * 8 + ring(z, d, 8)} for d in (1, -1)}
    yhdev = {"mp": (1 - yh) * 8 + z}
    peers = [{"mp": lax.rem(mp + d, 16)} for d in range(1, 16)]

    barrier = pltpu.get_barrier_semaphore()
    everyone = [sib, ydev, xdev[1], xdev[-1]] + peers
    for dev in everyone:
        pl.semaphore_signal(barrier, inc=1, device_id=dev, device_id_type=MESH)
    pl.semaphore_wait(barrier, len(everyone))

    started = []

    def send(src, dst, dev):
        n = len(started)
        cp = pltpu.make_async_remote_copy(
            src_ref=src, dst_ref=dst, send_sem=send_sem.at[n], recv_sem=recv_sem.at[n],
            device_id=dev, device_id_type=MESH,
        )
        cp.start()
        started.append(cp)
        return cp

    def wp(xd, yd, r0, n, core=None):
        core = c if core is None else core
        r = pl.multiple_of(core * depth + r0, 16)
        return wfull.at[ring(x, xd, 4) * 2 + yd, pl.ds(r, n), :]

    def wsend(xd, yd, r0, n, dev):
        return send(wp(xd, yd, r0, n), wp(xd, yd, r0, n), dev)

    def wown(r0, n, dev):
        return send(w_ref.at[pl.ds(r0, n), :], wp(0, y, r0, n), dev)

    def tp(yb, zd, r0=0, n=rows):
        return tfull.at[yb * 8 + ring(z, zd, 8), pl.ds(r0, n), :]

    def tsend(yb, zd, r0, n, dev):
        return send(tp(yb, zd, r0, n), tp(yb, zd, r0, n), dev)

    to_sib = []
    yo = 1 - y
    t_yh = send(tok_ref, tp(yh, 0), yhdev)
    t_own = {d: send(tok_ref, tp(yh, 0), zdev[d]) for d in (1, -1)}
    b_y = wown(half, half, ydev)
    a_x = {d: wown(0, half, xdev[d]) for d in (1, -1)}
    a_y = wown(0, half, ydev)
    b_x = {d: wown(half, half, xdev[d]) for d in (1, -1)}
    to_sib.append(wown(0, depth, sib))

    def column_to_rows(parts):
        lane = lax.broadcasted_iota(jnp.int32, (rows, 128), 1)
        tile = jnp.zeros((rows, 128), F32)
        for i, p in enumerate(parts):
            tile = jnp.where(lane == i, p, tile)
        return jnp.transpose(tile)[:8, :]

    def rows_to_columns(r):
        return jnp.transpose(jnp.concatenate([r, jnp.zeros((120, rows), F32)], axis=0))

    def exchange(which, parts):
        stat_out[which] = column_to_rows(parts)
        stat_in[which, mp] = stat_out[which]
        cps = []
        for d in range(1, 16):
            cp = pltpu.make_async_remote_copy(
                src_ref=stat_out.at[which], dst_ref=stat_in.at[which, mp],
                send_sem=stat_send.at[which, d], recv_sem=stat_recv.at[which, d],
                device_id=peers[d - 1], device_id_type=MESH,
            )
            cp.start()
            cps.append(cp)
        return cps

    own = tok_ref[...].astype(F32)
    local_mean = jnp.mean(own, axis=-1, keepdims=True)
    local_dev = own - local_mean
    stats = exchange(0, (local_mean, jnp.sum(local_dev * local_dev, axis=-1, keepdims=True)))
    tfull[mp] = tok_ref[...]
    wfull[x * 2 + y, pl.ds(pl.multiple_of(c * depth, 16), depth), :] = w_ref[...]

    t_in = {(0, d): t_own[d] for d in (1, -1)}
    t_yh.wait_recv()
    for d in (1, -1):
        t_in[(1, d)] = tsend(1 - yh, 0, 0, rows, zdev[d])

    def t_hop(h, rel):
        yb = yh if rel == 0 else 1 - yh
        for d in (1, -1):
            t_in[(rel, d)].wait_recv()
        for d in (1, -1):
            if h < 3:
                t_in[(rel, d)] = tsend(yb, -d * h, 0, rows, zdev[d])
            elif h == 3:
                t_in[(rel, d)] = tsend(yb, -d * h, 0 if d == 1 else hrow, hrow, zdev[d])

    t_hop(1, 0)
    b_y.wait_recv()
    bo_x = {d: wsend(0, yo, half, half, xdev[d]) for d in (1, -1)}
    to_sib.append(wsend(0, yo, half, half, sib))
    aq_x, ay_x = {}, {}
    for d in (1, -1):
        a_x[d].wait_recv()
        aq_x[d] = wsend(-d, y, 0 if d == 1 else quarter, quarter, xdev[d])
        ay_x[d] = wsend(-d, y, 0, half, ydev)
        to_sib.append(wsend(-d, y, 0, half, sib))
    t_hop(1, 1)
    a_y.wait_recv()
    to_sib.append(wsend(0, yo, 0, half, sib))
    bq_x, boq_x = {}, {}
    for d in (1, -1):
        b_x[d].wait_recv()
        bq_x[d] = wsend(-d, y, half + (0 if d == 1 else quarter), quarter, xdev[d])
        to_sib.append(wsend(-d, y, half, half, sib))
    t_hop(2, 0)
    ayq = {}
    for d in (1, -1):
        aq_x[d].wait_recv()
        r0 = 0 if d == 1 else quarter
        ayq[d] = wsend(-2 * d, y, r0, quarter, ydev)
        to_sib.append(wsend(-2 * d, y, r0, quarter, sib))
    t_hop(2, 1)
    for d in (1, -1):
        bo_x[d].wait_recv()
        boq_x[d] = wsend(-d, yo, half + (0 if d == 1 else quarter), quarter, xdev[d])
        to_sib.append(wsend(-d, yo, half, half, sib))
    t_hop(3, 0)
    for d in (1, -1):
        bq_x[d].wait_recv()
        to_sib.append(wsend(-2 * d, y, half + (0 if d == 1 else quarter), quarter, sib))
    for d in (1, -1):
        ay_x[d].wait_recv()
        to_sib.append(wsend(-d, yo, 0, half, sib))
    t_hop(3, 1)
    for d in (1, -1):
        boq_x[d].wait_recv()
        to_sib.append(wsend(-2 * d, yo, half + (0 if d == 1 else quarter), quarter, sib))
    for d in (1, -1):
        ayq[d].wait_recv()
        to_sib.append(wsend(-2 * d, yo, 0 if d == 1 else quarter, quarter, sib))

    for cp in stats:
        cp.wait_recv()
    means = stat_in[0, :, 0:1, :]
    mean_row = jnp.mean(means, axis=0)
    sq = jnp.sum(stat_in[0, :, 1:2, :], axis=0) + width * jnp.sum(
        (means - mean_row[None]) * (means - mean_row[None]), axis=0
    )
    inv_row = lax.rsqrt(sq / (16.0 * width) + EPS)
    both = rows_to_columns(jnp.concatenate([mean_row, inv_row, jnp.zeros((6, rows), F32)], axis=0))
    mean, inv = both[:, 0:1], both[:, 1:2]

    t_hop(4, 0)
    t_hop(4, 1)
    for cp in to_sib:
        cp.wait_recv()

    acc[...] = jnp.zeros_like(acc)

    @pl.loop(0, 8)
    def _(k):
        for s in range(2):
            unit = ((tfull[2 * k + s].astype(F32) - mean) * inv).astype(BF16)
            normed[k, :, s * width : (s + 1) * width] = unit
            normt[2 * k + s] = jnp.transpose(unit)
        acc[...] += mm(normed[k], wfull[k], ((1,), (0,)))

    qkv[...] = acc[...].astype(BF16)

    for h in range(2):
        base = 3 * h * HD
        parts = [qkv[:, base + i * HD : base + (i + 1) * HD] for i in range(3)]
        out, dq, dk, dv = one_head(*parts, og_ref[:, h * HD : (h + 1) * HD])
        att_ref[:, h * HD : (h + 1) * HD] = out.astype(BF16)
        for i, g in enumerate((dq, dk, dv)):
            dqkv[:, base + i * HD : base + (i + 1) * HD] = g.astype(BF16)

    def back(yb, zd):
        j = yb * 8 + ring(z, zd, 8)
        w = wfull[j // 2, pl.ds(pl.multiple_of((j % 2) * depth, 16), depth), :]
        bk[j] = mm(dqkv[...], w, ((1,), (1,))).astype(BF16)

    def bp(yb, zd, r0=0, n=rows):
        return bk.at[yb * 8 + ring(z, zd, 8), pl.ds(r0, n), :]

    ybs = (1 - yh, yh)
    b_in = {}

    def back_start():
        for r in range(2):
            back(ybs[r], 4)
            for i, d in enumerate((1, -1)):
                b_in[(r, d)] = send(bp(ybs[r], 4, i * hrow, hrow), bh.at[r, i], zdev[d])

    def back_hop(h, r):
        for i, d in enumerate((1, -1)):
            back(ybs[r], d * (4 - h))
        for i, d in enumerate((1, -1)):
            b_in[(r, d)].wait_recv()
            if h == 1:
                dst = bp(ybs[r], d * 3, i * hrow, hrow)
                dst[...] = (dst[...].astype(F32) + bh[r, i].astype(F32)).astype(BF16)
            else:
                dst = bp(ybs[r], d * (4 - h))
                dst[...] = (dst[...].astype(F32) + bw[r, i, h - 2].astype(F32)).astype(BF16)
            b_in[(r, d)] = send(bp(ybs[r], d * (4 - h)), bw.at[r, i, h - 1], zdev[d])

    g_sib = {}

    def chip(xd, yd):
        return ring(x, xd, 4) * 2 + yd

    def grad(xd, yd):
        q = chip(xd, yd)
        gout[q] = mm(normt[2 * q + 1 - c], dqkv[...], ((1,), (0,))).astype(BF16)
        g_sib[(xd, yd is yo)] = send(gout.at[q], gin.at[q], sib)
        gown[q] = mm(normt[2 * q + c], dqkv[...], ((1,), (0,))).astype(BF16)

    def join(xd, yd):
        q = chip(xd, yd)
        g_sib[(xd, yd is yo)].wait_recv()
        gown[q] = (gown[q].astype(F32) + gin[q].astype(F32)).astype(BF16)

    def gp(xd, yd, r0, n):
        return gown.at[chip(xd, yd), pl.ds(r0, n), :]

    def add(dst, src):
        dst[...] = (dst[...].astype(F32) + src[...].astype(F32)).astype(BF16)

    back_start()
    grad(2, yo)
    grad(2, y)
    back_hop(1, 0)
    grad(1, yo)
    grad(-1, yo)
    back_hop(1, 1)
    ga_y, gq, gh = {}, {}, {}
    for i, yd in enumerate((yo, y)):
        join(2, yd)
        if i == 0:
            ga_y[2] = send(gp(2, yo, 0, half), gya.at[0], ydev)
        for s, d in enumerate((1, -1)):
            gq[(i, d)] = send(gp(2, yd, half + s * quarter, quarter), gxq.at[i, s], xdev[d])
    grad(0, yo)
    for s, d in enumerate((1, -1)):
        join(d, yo)
        ga_y[d] = send(gp(d, yo, 0, half), gya.at[1 + s], ydev)
    grad(1, y)
    grad(-1, y)
    join(0, yo)
    ga_y[0] = send(gp(0, yo, 0, half), gya.at[3], ydev)
    back_hop(2, 0)
    for d in (1, -1):
        join(d, y)
    back_hop(2, 1)
    for i, yd in enumerate((yo, y)):
        for s, d in enumerate((1, -1)):
            gq[(i, d)].wait_recv()
            add(gp(d, yd, half + s * quarter, quarter), gxq.at[i, s])
            gh[(i, d)] = send(gp(d, yd, half, half), gxh.at[i, s], xdev[d])
    grad(0, y)
    join(0, y)
    ga_y[2].wait_recv()
    add(gp(2, y, 0, half), gya.at[0])
    for s, d in enumerate((1, -1)):
        gq[(2, d)] = send(gp(2, y, s * quarter, quarter), gxq.at[2, s], xdev[d])
    back_hop(3, 0)
    back_hop(3, 1)
    for s, d in enumerate((1, -1)):
        ga_y[d].wait_recv()
        add(gp(d, y, 0, half), gya.at[1 + s])
        gq[(2, d)].wait_recv()
        add(gp(d, y, s * quarter, quarter), gxq.at[2, s])
        gh[(2, d)] = send(gp(d, y, 0, half), gxh.at[2, s], xdev[d])
    for s, d in enumerate((1, -1)):
        gh[(0, d)].wait_recv()
        add(gp(0, yo, half, half), gxh.at[0, s])
    gb_y = send(gp(0, yo, half, half), gyb, ydev)
    ga_y[0].wait_recv()
    add(gp(0, y, 0, half), gya.at[3])

    back(ybs[0], 0)
    back(ybs[1], 0)
    for i, d in enumerate((1, -1)):
        b_in[(0, d)].wait_recv()
        add(bp(ybs[0], 0), bw.at[0, i, 2])
    b_y2 = send(bp(ybs[0], 0), by, yhdev)
    for i, d in enumerate((1, -1)):
        b_in[(1, d)].wait_recv()
    d_normed = (
        bk[mp].astype(F32) + bw[1, 0, 2].astype(F32) + bw[1, 1, 2].astype(F32)
    )
    b_y2.wait_recv()
    d_normed = d_normed + by[...].astype(F32)
    unit = (tok_ref[...].astype(F32) - mean) * inv
    stats2 = exchange(
        1,
        (
            jnp.sum(d_normed, axis=-1, keepdims=True),
            jnp.sum(d_normed * unit, axis=-1, keepdims=True),
        ),
    )

    for s, d in enumerate((1, -1)):
        gh[(1, d)].wait_recv()
        gh[(2, d)].wait_recv()
    gb_y.wait_recv()
    mine = chip(0, y)
    gw_ref[:half, :] = (
        gown[mine, :half, :].astype(F32) + gxh[2, 0].astype(F32) + gxh[2, 1].astype(F32)
    ).astype(BF16)
    gw_ref[half:, :] = (
        gown[mine, half:, :].astype(F32) + gxh[1, 0].astype(F32) + gxh[1, 1].astype(F32)
        + gyb[...].astype(F32)
    ).astype(BF16)

    for cp in stats2:
        cp.wait_recv()
    sums = rows_to_columns(jnp.sum(stat_in[1], axis=0)) * (1.0 / (16.0 * width))
    gt_ref[...] = inv * (d_normed - sums[:, 0:1] - unit * sums[:, 1:2])

    for cp in started + stats + stats2:
        cp.wait_send()


SENDS = 121


def per_device(tokens, w_qkv, out_grad):
    rows, width = tokens.shape
    depth, cols = w_qkv.shape
    half, quarter = depth // 2, depth // 4
    vmem = pltpu.VMEM
    scratch = [
        vmem((8, 2 * depth, cols), BF16),
        vmem((16, rows, width), BF16),
        vmem((8, rows, 2 * width), BF16),
        vmem((16, width, rows), BF16),
        vmem((rows, cols), F32),
        vmem((rows, cols), BF16),
        vmem((rows, cols), BF16),
        vmem((8, depth, cols), BF16),
        vmem((8, depth, cols), BF16),
        vmem((8, depth, cols), BF16),
        vmem((4, half, cols), BF16),
        vmem((3, 2, quarter, cols), BF16),
        vmem((3, 2, half, cols), BF16),
        vmem((half, cols), BF16),
        vmem((16, rows, width), BF16),
        vmem((2, 2, rows // 2, width), BF16),
        vmem((2, 2, 3, rows, width), BF16),
        vmem((rows, width), BF16),
        vmem((2, 8, rows), F32),
        vmem((2, 16, 8, rows), F32),
        pltpu.SemaphoreType.DMA((SENDS,)),
        pltpu.SemaphoreType.DMA((SENDS,)),
        pltpu.SemaphoreType.DMA((2, 16)),
        pltpu.SemaphoreType.DMA((2, 16)),
    ]
    return pl.pallas_call(
        kernel,
        out_shape=(
            jax.ShapeDtypeStruct(out_grad.shape, BF16),
            jax.ShapeDtypeStruct(tokens.shape, F32),
            jax.ShapeDtypeStruct(w_qkv.shape, BF16),
        ),
        in_specs=[pl.BlockSpec(memory_space=vmem)] * 3,
        out_specs=(pl.BlockSpec(memory_space=vmem),) * 3,
        scratch_shapes=scratch,
        compiler_params=pltpu.CompilerParams(
            collective_id=0, has_side_effects=True, vmem_limit_bytes=62 * 1024 * 1024
        ),
    )(tokens, w_qkv, out_grad)


def solution(mesh):
    placed = (P("dp", "mp"), P("dp", "mp"), P("dp", "mp"))
    return jax.shard_map(
        per_device, mesh=mesh, in_specs=placed, out_specs=placed, check_vma=False
    )
```

```python
import jax
import jax.numpy as jnp
from jax import lax
from jax.experimental import pallas as pl
from jax.experimental.pallas import tpu as pltpu
from jax.sharding import PartitionSpec as P

HD = 128
EPS = 1e-06
F32 = jnp.float32
BF16 = jnp.bfloat16
MESH = pl.DeviceIdType.MESH
SIGN = {"+": 1, "-": -1}
OTHER = {"+": "-", "-": "+"}

ORDER = (
    37, 6, 23, 87, 7, 56, 38, 39, 5, 55,
    8, 21, 57, 22, 24, 1, 2, 0, 25, 40,
    88, 59, 45, 13, 27, 58, 41, 62, 11, 48,
    52, 73, 75, 9, 60, 46, 66, 3, 69, 14,
    29, 30, 42, 63, 35, 15, 53, 77, 79, 49,
    4, 61, 47, 19, 26, 32, 67, 70, 28, 16,
    33, 64, 81, 43, 12, 54, 50, 83, 10, 17,
    31, 68, 71, 85, 89, 136, 144, 108, 36, 134,
    132, 102, 104, 140, 65, 112, 106, 114, 44, 110,
    18, 130, 142, 116, 34, 20, 51, 72, 138, 95,
    92, 93, 97, 91, 90, 94, 96, 98, 179, 105,
    109, 139, 169, 111, 107, 180, 137, 152, 164, 172,
    99, 170, 145, 131, 153, 146, 133, 173, 174, 141,
    147, 115, 177, 135, 143, 167, 175, 189, 154, 178,
    155, 181, 100, 168, 103, 183, 148, 118, 165, 149,
    124, 117, 119, 125, 162, 113, 156, 74, 171, 157,
    76, 163, 182, 150, 151, 120, 184, 176, 121, 191,
    126, 127, 78, 160, 80, 166, 188, 158, 185, 190,
    122, 123, 128, 82, 129, 84, 193, 86, 101, 159,
    161, 186, 192, 187,
)


def mm(a, b, dims, precision=None):
    return lax.dot_general(
        a, b, (dims, ((), ())), preferred_element_type=F32, precision=precision
    )


def normalize(v):
    centred = v - jnp.mean(v, axis=-1, keepdims=True)
    inv = lax.rsqrt(jnp.mean(centred * centred, axis=-1, keepdims=True) + EPS)
    return centred * inv, inv


def normalize_back(d, unit, inv):
    return inv * (
        d
        - jnp.mean(d, axis=-1, keepdims=True)
        - unit * jnp.mean(d * unit, axis=-1, keepdims=True)
    )


def one_head(q, k, v, og):
    qu, qi = normalize(q.astype(F32))
    ku, ki = normalize(k.astype(F32))
    scale = 1.0 / (HD**0.5)
    scores = mm(qu, ku, ((1,), (1,)), lax.Precision.HIGHEST) * scale
    weights = jnp.exp(scores)
    probs = weights / jnp.sum(weights, axis=-1, keepdims=True)
    probs16 = probs.astype(BF16)
    out = mm(probs16, v, ((1,), (0,)))
    dv = mm(probs16, og, ((0,), (0,)))
    dp = mm(og, v, ((1,), (1,)))
    ds = (probs * (dp - jnp.sum(dp * probs, axis=-1, keepdims=True)) * scale).astype(BF16)
    dq = normalize_back(mm(ds, ku.astype(BF16), ((1,), (0,))), qu, qi)
    dk = normalize_back(mm(ds, qu.astype(BF16), ((0,), (0,))), ku, ki)
    return out, dq, dk, dv


def split_rows(depth):
    a = depth * 3 // 8
    ap = depth * 5 // 24
    bp = depth * 7 // 24
    return {
        "A": (0, a),
        "B": (a, depth - a),
        "A+": (0, ap),
        "A-": (ap, a - ap),
        "B+": (a, bp),
        "B-": (a + bp, depth - a - bp),
    }


def kernel(
    tok_hbm, w_hbm, og_hbm,
    att_hbm, gt_hbm, gw_hbm,
    og_ref, att_ref, gt_ref, gw_ref, load_sem, store_sem,
    wfull, tfull, normed, normt, acc, dqkv, cols,
    gown, gout, gin, gya, gaq, gaf, gad, gbq, gbf, gbd, gyb,
    bk, bin, by, st_own, st_peer, st_ring,
    send_sem, recv_sem,
):
    dp, mp = lax.axis_index("dp"), lax.axis_index("mp")
    x, y, c = dp // 4, (dp // 2) % 2, dp % 2
    yh, z = mp // 8, mp % 8
    rows, width = tok_hbm.shape
    depth = w_hbm.shape[0]
    hrow = rows // 2
    part = split_rows(depth)

    def ring(v, d, n):
        return lax.rem(v + d + n, n)

    sib = {"dp": dp + 1 - 2 * c}
    ydev = {"dp": x * 4 + (1 - y) * 2 + c}
    xdev = {s: {"dp": ring(x, d, 4) * 4 + y * 2 + c} for s, d in SIGN.items()}
    zdev = {s: {"mp": yh * 8 + ring(z, d, 8)} for s, d in SIGN.items()}
    yhdev = {"mp": (1 - yh) * 8 + z}

    own_tok = tfull.at[mp]
    own_w = wfull.at[x * 2 + y, pl.ds(pl.multiple_of(c * depth, 16), depth), :]
    loads = [
        pltpu.make_async_copy(src, dst, load_sem.at[i])
        for i, (src, dst) in enumerate(((tok_hbm, own_tok), (w_hbm, own_w), (og_hbm, og_ref)))
    ]
    stores = []

    def store(src, dst):
        cp = pltpu.make_async_copy(src, dst, store_sem.at[len(stores)])
        cp.start()
        stores.append(cp)

    copies = {}
    steps = {}

    def send(name, src, dst, dev):
        n = len(copies)
        cp = pltpu.make_async_remote_copy(
            src_ref=src, dst_ref=dst, send_sem=send_sem.at[n], recv_sem=recv_sem.at[n],
            device_id=dev, device_id_type=MESH,
        )
        cp.start()
        copies[name] = cp

    def wait(*names):
        for name in names:
            copies[name].wait_recv()

    def step(name):
        def keep(f):
            steps[name] = f
        return keep

    ys = {"y": y, "n": 1 - y}

    def wp(xd, yd, rng):
        r = pl.multiple_of(c * depth + rng[0], 16)
        return wfull.at[ring(x, xd, 4) * 2 + ys[yd], pl.ds(r, rng[1]), :]

    def wown(name, rng, dev):
        send(name, w_hbm.at[pl.ds(*rng), :], wp(0, "y", rng), dev)

    def wsend(name, xd, yd, rng, dev):
        send(name, wp(xd, yd, rng), wp(xd, yd, rng), dev)

    @step("iS")
    def _():
        wown("S0y", (0, depth), sib)

    @step("iBy")
    def _():
        wown("By", part["B"], ydev)

    @step("iAy")
    def _():
        wown("Ay", part["A"], ydev)

    @step("fBy")
    def _():
        wait("By")
        for p, s in (("+", "+"), ("-", "-"), ("-", "+"), ("+", "-")):
            wsend("Bo" + p + s, 0, "n", part["B" + p], xdev[s])
        wsend("SBy", 0, "n", part["B"], sib)

    @step("fAy")
    def _():
        wait("Ay")
        wsend("SAy", 0, "n", part["A"], sib)

    def weight_start(k, p, s):
        @step("i" + k + p + s)
        def _():
            wown(k + p + s, part[k + p], xdev[s])

    def weight_steps(s, d):
        o = OTHER[s]

        def a_piece(p):
            @step("fA" + p + s)
            def _():
                wait("A" + p + s)
                if p == s:
                    wsend("Aq" + s, -d, "y", part["A" + s], xdev[s])
                wsend("Ay" + p + s, -d, "y", part["A" + p], ydev)
                wsend("SA" + p + s, -d, "y", part["A" + p], sib)

            @step("fAy" + p + s)
            def _():
                wait("Ay" + p + s)
                wsend("SAy" + p + s, -d, "n", part["A" + p], sib)

        def b_piece(b, yd):
            @step("f" + b + s + s)
            def _():
                wait(b + s + s)
                wsend(b + "q" + s, -d, yd, part["B" + s], xdev[s])

            @step("f" + b + o + s)
            def _():
                wait(b + o + s)
                wsend("S" + b + s, -d, yd, part["B"], sib)

            @step("f" + b + "q" + s)
            def _():
                wait(b + "q" + s)
                wsend("S" + b + "q" + s, -2 * d, yd, part["B" + s], sib)

        a_piece(s)
        a_piece(o)
        b_piece("B", "y")
        b_piece("Bo", "n")

        @step("fAq" + s)
        def _():
            wait("Aq" + s)
            wsend("Ayq" + s, -2 * d, "y", part["A" + s], ydev)
            wsend("SAq" + s, -2 * d, "y", part["A" + s], sib)

        @step("fAyq" + s)
        def _():
            wait("Ayq" + s)
            wsend("SAyq" + s, -2 * d, "n", part["A" + s], sib)

    for s, d in SIGN.items():
        for p in SIGN:
            weight_start("A", p, s)
            weight_start("B", p, s)
        weight_steps(s, d)

    yb = {"o": yh, "p": 1 - yh}

    def feature(r, zd):
        return yb[r] * 8 + ring(z, zd, 8)

    def tp(r, zd, i):
        return tfull.at[feature(r, zd), pl.ds(i * hrow, hrow), :]

    def is_long(i, s):
        return (i == 0) == (s == "+")

    def token_start(i):
        mine = tok_hbm.at[pl.ds(i * hrow, hrow), :]

        @step("iTh%d" % i)
        def _():
            send("Th%d" % i, mine, tp("o", 0, i), yhdev)

        def along(s):
            @step("iT%d%s" % (i, s))
            def _():
                send("To%d0%s" % (i, s), mine, tp("o", 0, i), zdev[s])

        for s in SIGN:
            along(s)

        @step("fTP%d" % i)
        def _():
            wait("Th%d" % i)
            for s in SIGN:
                send("Tp%d0%s" % (i, s), tp("p", 0, i), tp("p", 0, i), zdev[s])

    def token_hop(r, i, h, s, d):
        @step("fT%s%d%d%s" % (r, i, h, s))
        def _():
            wait("T%s%d%d%s" % (r, i, h - 1, s))
            if h < 3 + is_long(i, s):
                src = tp(r, -d * h, i)
                send("T%s%d%d%s" % (r, i, h, s), src, src, zdev[s])

    for i in range(2):
        token_start(i)
        for r in "op":
            for s, d in SIGN.items():
                for h in range(1, 4 + is_long(i, s)):
                    token_hop(r, i, h, s, d)

    def as_rows(parts):
        lane = lax.broadcasted_iota(jnp.int32, (rows, 128), 1)
        tile = jnp.zeros((rows, 128), F32)
        for i, p in enumerate(parts):
            tile = jnp.where(lane == i, p, tile)
        return jnp.transpose(tile)[:8, :]

    def as_columns(parts):
        pad = jnp.zeros((128 - len(parts), rows), F32)
        return jnp.transpose(jnp.concatenate(list(parts) + [pad], axis=0))

    def stat_send(which, name, s):
        send(name, st_ring.at[which, z], st_ring.at[which, z], zdev[s])

    def stat_hop(which, p, h, s, d):
        @step("%sS%d%s" % ("fb"[which], h, s))
        def _():
            wait("%st%d%s" % (p, h - 1, s))
            if h < 3 or (h == 3 and d == 1):
                src = st_ring.at[which, ring(z, -d * h, 8)]
                send("%st%d%s" % (p, h, s), src, src, zdev[s])

    for h in range(1, 5):
        for s, d in SIGN.items():
            if h < 4 or d == 1:
                stat_hop(0, "S", h, s, d)
                stat_hop(1, "R", h, s, d)

    @step("iSt")
    def _():
        loads[0].wait()
        own = own_tok[...].astype(F32)
        mean = jnp.mean(own, axis=-1, keepdims=True)
        dev = own - mean
        st_own[0] = as_rows((mean, jnp.sum(dev * dev, axis=-1, keepdims=True)))
        send("Sth", st_own.at[0], st_peer.at[0], yhdev)

    @step("fSt")
    def _():
        wait("Sth")
        a, b = st_own[0], st_peer[0]
        gap = a[0:1] - b[0:1]
        st_ring[0, z] = jnp.concatenate(
            [
                0.5 * (a[0:1] + b[0:1]),
                a[1:2] + b[1:2] + (0.5 * width) * gap * gap,
                jnp.zeros((6, rows), F32),
            ],
            axis=0,
        )
        for s in SIGN:
            stat_send(0, "St0" + s, s)

    @step("stat")
    def _():
        got = st_ring[0]
        means = got[:, 0:1, :]
        mean = jnp.mean(means, axis=0)
        gap = means - mean[None]
        sq = jnp.sum(got[:, 1:2, :], axis=0) + (2.0 * width) * jnp.sum(gap * gap, axis=0)
        cols[0] = as_columns((mean, lax.rsqrt(sq / (16.0 * width) + EPS)))
        normed[:, rows:, :] = jnp.ones_like(normed[:, rows:, :])
        acc[...] = jnp.zeros_like(acc)

    def norm_block(r, zd):
        @step("n%s%d" % (r, zd))
        def _():
            j = feature(r, zd)
            unit = (tfull[j].astype(F32) - cols[0, :, 0:1]) * cols[0, :, 1:2]
            unit = unit.astype(BF16)
            lanes = pl.ds(pl.multiple_of((j % 2) * width, 128), width)
            normed[j // 2, :rows, lanes] = unit
            normt[j] = jnp.transpose(unit)

    def product(xd, yd, waits):
        @step("m%d%s" % (xd, yd))
        def _():
            wait(*waits)
            if (xd, yd) == (0, "y"):
                loads[1].wait()
            k = ring(x, xd, 4) * 2 + ys[yd]
            acc[...] += mm(normed[k], wfull[k], ((1,), (0,)))

    product(0, "y", ("S0y",))
    product(0, "n", ("SBy", "SAy"))
    for s, d in SIGN.items():
        product(-d, "y", ("SA+" + s, "SA-" + s, "SB" + s))
        product(-d, "n", ("SAy+" + s, "SAy-" + s, "SBo" + s))
    product(2, "y", ("SAq+", "SAq-", "SBq+", "SBq-"))
    product(2, "n", ("SAyq+", "SAyq-", "SBoq+", "SBoq-"))

    @step("att")
    def _():
        loads[2].wait()
        for h in range(2):
            base = 3 * h * HD
            at = [slice(base + i * HD, base + (i + 1) * HD) for i in range(3)]
            qkv = [acc[:rows, a].astype(BF16) for a in at]
            mine = slice(h * HD, (h + 1) * HD)
            out, dq, dk, dv = one_head(*qkv, og_ref[:, mine])
            att_ref[:, mine] = out.astype(BF16)
            for a, g in zip(at, (dq, dk, dv)):
                dqkv[:, a] = g.astype(BF16)
        store(att_ref, att_hbm)

    @step("bSt")
    def _():
        d = dqkv[...].astype(F32)
        st_own[1] = as_rows(
            (
                jnp.sum(d * acc[rows : rows + 1, :], axis=-1, keepdims=True),
                jnp.sum(d * acc[:rows, :], axis=-1, keepdims=True),
            )
        )
        send("Rth", st_own.at[1], st_peer.at[1], yhdev)

    @step("bSh")
    def _():
        wait("Rth")
        st_ring[1, z] = st_own[1] + st_peer[1]
        for s in SIGN:
            stat_send(1, "Rt0" + s, s)

    @step("bstat")
    def _():
        sums = jnp.sum(st_ring[1], axis=0) * (1.0 / (16.0 * width))
        cols[1] = as_columns((sums[0:1], sums[1:2]))

    def bp(r, zd, i):
        return bk.at[feature(r, zd), pl.ds(i * hrow, hrow), :]

    def add(dst, *srcs):
        total = dst[...].astype(F32)
        for src in srcs:
            total = total + src[...].astype(F32)
        dst[...] = total.astype(BF16)

    def back(r, zd):
        @step("c%s%d" % (r, zd))
        def _():
            j = feature(r, zd)
            w = wfull[j // 2, pl.ds(pl.multiple_of((j % 2) * depth, 16), depth), :]
            bk[j] = mm(dqkv[...], w, ((1,), (1,))).astype(BF16)
            if zd == 4:
                back_send(r, 0, 0, "+", 4)
                back_send(r, 1, 0, "-", 4)

    def back_send(r, i, h, s, zd):
        dst = bin.at["op".index(r), i, "+-".index(s), h]
        send("K%s%d%d%s" % (r, i, h, s), bp(r, zd, i), dst, zdev[s])

    def got(r, i, h, s):
        return bin.at["op".index(r), i, "+-".index(s), h]

    def back_hop(r, i, h, s, d):
        @step("k%s%d%d%s" % (r, i, h, s))
        def _():
            zd = d * (4 - h)
            if h > 1 or is_long(i, s):
                wait("K%s%d%d%s" % (r, i, h - 1, s))
                add(bp(r, zd, i), got(r, i, h - 1, s))
            back_send(r, i, h, s, zd)

    for r in "op":
        for zd in (0, 1, 2, 3, 4, -1, -2, -3):
            norm_block(r, zd)
            back(r, zd)
        for i in range(2):
            for h in (1, 2, 3):
                for s, d in SIGN.items():
                    back_hop(r, i, h, s, d)

    def back_end(i):
        mine = pl.ds(i * hrow, hrow)

        @step("kp%d" % i)
        def _():
            wait("Kp%d3+" % i, "Kp%d3-" % i)
            add(bp("p", 0, i), got("p", i, 3, "+"), got("p", i, 3, "-"))
            send("Kh%d" % i, bp("p", 0, i), by.at[mine, :], yhdev)

        @step("ft%d" % i)
        def _():
            wait("Ko%d3+" % i, "Ko%d3-" % i, "Kh%d" % i)
            total = bp("o", 0, i)[...].astype(F32) + by[mine, :].astype(F32)
            for s in SIGN:
                total = total + got("o", i, 3, s)[...].astype(F32)
            mean, inv = cols[0, mine, 0:1], cols[0, mine, 1:2]
            unit = (tp("o", 0, i)[...].astype(F32) - mean) * inv
            gt_ref[mine, :] = inv * (total - cols[1, mine, 0:1] - unit * cols[1, mine, 1:2])
            store(gt_ref.at[mine, :], gt_hbm.at[mine, :])

    back_end(0)
    back_end(1)

    def chip(xd, yd):
        return ring(x, xd, 4) * 2 + ys[yd]

    def gp(xd, yd, rng):
        return gown.at[chip(xd, yd), pl.ds(*rng), :]

    XS = (0, 1, -1, 2)
    TOWARD = {1: "+", -1: "-"}

    def grad(xd, yd):
        @step("g%d%s" % (xd, yd))
        def _():
            q = chip(xd, yd)
            gout[q] = mm(normt[2 * q + 1 - c], dqkv[...], ((1,), (0,))).astype(BF16)
            send("G%d%s" % (xd, yd), gout.at[q], gin.at[q], sib)
            gown[q] = mm(normt[2 * q + c], dqkv[...], ((1,), (0,))).astype(BF16)

        @step("j%d%s" % (xd, yd))
        def _():
            wait("G%d%s" % (xd, yd))
            q = chip(xd, yd)
            add(gown.at[q], gin.at[q])
            if yd == "n":
                send("Y%d" % xd, gp(xd, "n", part["A"]), gya.at[XS.index(xd)], ydev)
            yi = "yn".index(yd)
            if xd == 2:
                for s in SIGN:
                    send("BQ" + yd + s, gp(2, yd, part["B" + s]), gbq[s].at[yi], xdev[s])
            elif xd != 0:
                s = TOWARD[xd]
                p = OTHER[s]
                send("BF" + yd + s, gp(xd, yd, part["B" + p]), gbf[p].at[yi], xdev[s])

    def sum_y(xd):
        @step("ya%d" % xd)
        def _():
            wait("Y%d" % xd)
            add(gp(xd, "y", part["A"]), gya.at[XS.index(xd)])
            if xd == 2:
                for s in SIGN:
                    send("AQ" + s, gp(2, "y", part["A" + s]), gaq[s], xdev[s])
            elif xd != 0:
                s = TOWARD[xd]
                p = OTHER[s]
                send("AF" + s, gp(xd, "y", part["A" + p]), gaf[p], xdev[s])

    def sum_x(s, d):
        def along(yd):
            yi = "yn".index(yd)

            @step("bh" + yd + s)
            def _():
                wait("BQ" + yd + s)
                add(gp(d, yd, part["B" + s]), gbq[s].at[yi])
                send("BD" + yd + s, gp(d, yd, part["B" + s]), gbd[s].at[yi], xdev[s])

        along("y")
        along("n")

        @step("ah" + s)
        def _():
            wait("AQ" + s)
            add(gp(d, "y", part["A" + s]), gaq[s])
            send("AD" + s, gp(d, "y", part["A" + s]), gad[s], xdev[s])

        @step("bn" + s)
        def _():
            wait("BDn" + s, "BFn" + OTHER[s])
            add(gp(0, "n", part["B" + s]), gbd[s].at[1], gbf[s].at[1])
            send("Yb" + s, gp(0, "n", part["B" + s]), gyb[s], ydev)

        def finish(rng, *terms):
            total = gp(0, "y", rng)[...].astype(F32)
            for t in terms:
                total = total + t[...].astype(F32)
            mine = pl.ds(*rng)
            gw_ref[mine, :] = total.astype(BF16)
            store(gw_ref.at[mine, :], gw_hbm.at[mine, :])

        @step("fgA" + s)
        def _():
            wait("AD" + s, "AF" + OTHER[s])
            finish(part["A" + s], gad[s], gaf[s])

        @step("fgB" + s)
        def _():
            wait("BDy" + s, "BFy" + OTHER[s], "Yb" + s)
            finish(part["B" + s], gbd[s].at[0], gbf[s].at[0], gyb[s])

    for xd in XS:
        grad(xd, "y")
        grad(xd, "n")
        sum_y(xd)
    for s, d in SIGN.items():
        sum_x(s, d)

    for cp in loads:
        cp.start()
    barrier = pltpu.get_barrier_semaphore()
    everyone = [sib, ydev, xdev["+"], xdev["-"], zdev["+"], zdev["-"], yhdev]
    for dev in everyone:
        pl.semaphore_signal(barrier, inc=1, device_id=dev, device_id_type=MESH)
    pl.semaphore_wait(barrier, len(everyone))

    todo = list(steps.values())
    assert sorted(ORDER) == list(range(len(todo)))
    for n in ORDER:
        todo[n]()
    assert len(copies) == COPIES
    for cp in copies.values():
        cp.wait_send()
    for cp in stores:
        cp.wait()


COPIES = 157


def hand_over(*refs):
    for src, dst in zip(refs[:3], refs[3:]):
        dst[...] = src[...]


def per_device(tokens, w_qkv, out_grad):
    rows, width = tokens.shape
    depth, wide = w_qkv.shape
    part = split_rows(depth)
    vmem = pltpu.VMEM

    def count(name):
        return part[name][1]

    a_part = {s: vmem((count("A" + s), wide), BF16) for s in SIGN}
    b_part = {s: vmem((count("B" + s), wide), BF16) for s in SIGN}
    b_pair = {s: vmem((2, count("B" + s), wide), BF16) for s in SIGN}
    scratch = [
        vmem(out_grad.shape, BF16),
        vmem(out_grad.shape, BF16),
        vmem(tokens.shape, F32),
        vmem(w_qkv.shape, BF16),
        pltpu.SemaphoreType.DMA((3,)),
        pltpu.SemaphoreType.DMA((7,)),
        vmem((8, 2 * depth, wide), BF16),
        vmem((16, rows, width), BF16),
        vmem((8, rows + 16, 2 * width), BF16),
        vmem((16, width, rows), BF16),
        vmem((rows + 16, wide), F32),
        vmem((rows, wide), BF16),
        vmem((2, rows, 128), F32),
        vmem((8, depth, wide), BF16),
        vmem((8, depth, wide), BF16),
        vmem((8, depth, wide), BF16),
        vmem((4, count("A"), wide), BF16),
        a_part, a_part, a_part, b_pair, b_pair, b_pair, b_part,
        vmem((16, rows, width), BF16),
        vmem((2, 2, 2, 4, rows // 2, width), BF16),
        vmem((rows, width), BF16),
        vmem((2, 8, rows), F32),
        vmem((2, 8, rows), F32),
        vmem((2, 8, 8, rows), F32),
        pltpu.SemaphoreType.DMA((COPIES,)),
        pltpu.SemaphoreType.DMA((COPIES,)),
    ]
    anywhere = pl.BlockSpec(memory_space=pl.ANY)
    results = pl.pallas_call(
        kernel,
        out_shape=(
            jax.ShapeDtypeStruct(out_grad.shape, BF16),
            jax.ShapeDtypeStruct(tokens.shape, F32),
            jax.ShapeDtypeStruct(w_qkv.shape, BF16),
        ),
        in_specs=[anywhere] * 3,
        out_specs=(anywhere,) * 3,
        scratch_shapes=scratch,
        compiler_params=pltpu.CompilerParams(
            collective_id=0, has_side_effects=True, vmem_limit_bytes=62 * 1024 * 1024
        ),
    )(tokens, w_qkv, out_grad)
    in_vmem = [pl.BlockSpec(memory_space=vmem)] * 3
    return pl.pallas_call(
        hand_over,
        out_shape=[jax.ShapeDtypeStruct(r.shape, r.dtype) for r in results],
        in_specs=in_vmem,
        out_specs=in_vmem,
    )(*results)


def solution(mesh):
    placed = (P("dp", "mp"), P("dp", "mp"), P("dp", "mp"))
    return jax.shard_map(
        per_device, mesh=mesh, in_specs=placed, out_specs=placed, check_vma=False
    )
```

```python
import jax
import jax.numpy as jnp
from jax import lax
from jax.experimental import pallas as pl
from jax.experimental.pallas import tpu as pltpu
from jax.sharding import PartitionSpec as P

HD = 128
EPS = 1e-06
F32 = jnp.float32
BF16 = jnp.bfloat16
MESH = pl.DeviceIdType.MESH
SIGN = {"+": 1, "-": -1}
OTHER = {"+": "-", "-": "+"}

ORDER = (
    39, 57, 38, 5, 24, 21, 87, 37, 55, 1,
    56, 7, 22, 8, 23, 0, 2, 6, 45, 41,
    88, 9, 62, 59, 29, 40, 11, 46, 42, 75,
    73, 58, 27, 63, 60, 30, 52, 48, 13, 14,
    25, 47, 43, 79, 77, 3, 69, 19, 66, 31,
    64, 61, 4, 15, 35, 53, 49, 83, 10, 44,
    70, 81, 16, 12, 32, 65, 67, 28, 54, 50,
    85, 89, 113, 143, 125, 149, 139, 123, 17, 151,
    71, 121, 145, 33, 115, 68, 153, 26, 141, 117,
    111, 92, 94, 20, 100, 96, 51, 34, 90, 102,
    18, 98, 36, 119, 72, 147, 101, 97, 95, 99,
    91, 93, 103, 104, 105, 106, 195, 196, 107, 148,
    203, 197, 202, 181, 154, 124, 200, 199, 182, 144,
    146, 204, 161, 142, 156, 189, 108, 183, 201, 188,
    155, 162, 174, 175, 120, 152, 192, 150, 185, 122,
    193, 190, 207, 112, 158, 176, 205, 194, 178, 179,
    140, 109, 172, 157, 116, 164, 186, 198, 171, 114,
    180, 187, 163, 213, 118, 133, 74, 127, 126, 173,
    134, 128, 184, 160, 159, 76, 165, 166, 212, 209,
    191, 214, 135, 136, 78, 206, 130, 129, 208, 177,
    167, 80, 169, 215, 137, 138, 82, 132, 131, 84,
    211, 86, 110, 170, 210, 168, 217, 216,
)


def mm(a, b, dims):
    return lax.dot_general(a, b, (dims, ((), ())), preferred_element_type=F32)


def normalize(v):
    centred = v - jnp.mean(v, axis=-1, keepdims=True)
    inv = lax.rsqrt(jnp.mean(centred * centred, axis=-1, keepdims=True) + EPS)
    return centred * inv, inv


def normalize_back(d, unit, inv):
    return inv * (
        d
        - jnp.mean(d, axis=-1, keepdims=True)
        - unit * jnp.mean(d * unit, axis=-1, keepdims=True)
    )


def split(v, which):
    high = v.astype(BF16)
    low = (v - high.astype(F32)).astype(BF16)
    return jnp.concatenate((high, high, low) if which else (high, low, high), axis=1)


def one_head(q, k, v, og):
    qu, qi = normalize(q.astype(F32))
    ku, ki = normalize(k.astype(F32))
    scale = 1.0 / (HD**0.5)
    scores = mm(split(qu, 0), split(ku, 1), ((1,), (1,))) * scale
    weights = jnp.exp(scores)
    probs = weights / jnp.sum(weights, axis=-1, keepdims=True)
    probs16 = probs.astype(BF16)
    out = mm(probs16, v, ((1,), (0,)))
    dv = mm(probs16, og, ((0,), (0,)))
    dp = mm(og, v, ((1,), (1,)))
    ds = (probs * (dp - jnp.sum(dp * probs, axis=-1, keepdims=True)) * scale).astype(BF16)
    dq = normalize_back(mm(ds, ku.astype(BF16), ((1,), (0,))), qu, qi)
    dk = normalize_back(mm(ds, qu.astype(BF16), ((0,), (0,))), ku, ki)
    return out, dq, dk, dv


def split_rows(depth):
    a = depth * 3 // 8
    ap = depth * 5 // 24
    bp = depth * 7 // 24
    return {
        "A": (0, a),
        "B": (a, depth - a),
        "A+": (0, ap),
        "A-": (ap, a - ap),
        "B+": (a, bp),
        "B-": (a + bp, depth - a - bp),
    }


def kernel(
    tok_hbm, w_hbm, og_hbm,
    att_hbm, gt_hbm, gw_hbm,
    og_ref, att_ref, gt_ref, gw_ref, load_sem, store_sem,
    wfull, tfull, normed, normt, acc, dqkv, cols,
    gown, gout, gin, gya, gaq, gaf, gad, gbq, gbf, gbd, gyb,
    bk, bin, by, st_own, st_peer, st_ring,
    send_sem, recv_sem,
):
    dp, mp = lax.axis_index("dp"), lax.axis_index("mp")
    x, y, c = dp // 4, (dp // 2) % 2, dp % 2
    yh, z = mp // 8, mp % 8
    rows, width = tok_hbm.shape
    depth = w_hbm.shape[0]
    hrow = rows // 2
    part = split_rows(depth)

    def ring(v, d, n):
        return lax.rem(v + d + n, n)

    sib = {"dp": dp + 1 - 2 * c}
    ydev = {"dp": x * 4 + (1 - y) * 2 + c}
    xdev = {s: {"dp": ring(x, d, 4) * 4 + y * 2 + c} for s, d in SIGN.items()}
    zdev = {s: {"mp": yh * 8 + ring(z, d, 8)} for s, d in SIGN.items()}
    yhdev = {"mp": (1 - yh) * 8 + z}

    own_tok = tfull.at[mp]
    own_w = wfull.at[x * 2 + y, pl.ds(pl.multiple_of(c * depth, 16), depth), :]
    loads = [
        pltpu.make_async_copy(src, dst, load_sem.at[i])
        for i, (src, dst) in enumerate(((tok_hbm, own_tok), (w_hbm, own_w), (og_hbm, og_ref)))
    ]
    stores = []

    def store(src, dst):
        cp = pltpu.make_async_copy(src, dst, store_sem.at[len(stores)])
        cp.start()
        stores.append(cp)

    copies = {}
    steps = {}

    def send(name, src, dst, dev):
        n = len(copies)
        cp = pltpu.make_async_remote_copy(
            src_ref=src, dst_ref=dst, send_sem=send_sem.at[n], recv_sem=recv_sem.at[n],
            device_id=dev, device_id_type=MESH,
        )
        cp.start()
        copies[name] = cp

    def wait(*names):
        for name in names:
            copies[name].wait_recv()

    def step(name):
        def keep(f):
            steps[name] = f
        return keep

    ys = {"y": y, "n": 1 - y}

    def wp(xd, yd, rng):
        r = pl.multiple_of(c * depth + rng[0], 16)
        return wfull.at[ring(x, xd, 4) * 2 + ys[yd], pl.ds(r, rng[1]), :]

    def wown(name, rng, dev):
        send(name, w_hbm.at[pl.ds(*rng), :], wp(0, "y", rng), dev)

    def wsend(name, xd, yd, rng, dev):
        send(name, wp(xd, yd, rng), wp(xd, yd, rng), dev)

    @step("iS")
    def _():
        wown("S0y", (0, depth), sib)

    @step("iBy")
    def _():
        wown("By", part["B"], ydev)

    @step("iAy")
    def _():
        wown("Ay", part["A"], ydev)

    @step("fBy")
    def _():
        wait("By")
        for p, s in (("+", "+"), ("-", "-"), ("-", "+"), ("+", "-")):
            wsend("Bo" + p + s, 0, "n", part["B" + p], xdev[s])
        wsend("SBy", 0, "n", part["B"], sib)

    @step("fAy")
    def _():
        wait("Ay")
        wsend("SAy", 0, "n", part["A"], sib)

    def weight_start(k, p, s):
        @step("i" + k + p + s)
        def _():
            wown(k + p + s, part[k + p], xdev[s])

    def weight_steps(s, d):
        o = OTHER[s]

        def a_piece(p):
            @step("fA" + p + s)
            def _():
                wait("A" + p + s)
                if p == s:
                    wsend("Aq" + s, -d, "y", part["A" + s], xdev[s])
                wsend("Ay" + p + s, -d, "y", part["A" + p], ydev)
                wsend("SA" + p + s, -d, "y", part["A" + p], sib)

            @step("fAy" + p + s)
            def _():
                wait("Ay" + p + s)
                wsend("SAy" + p + s, -d, "n", part["A" + p], sib)

        def b_piece(b, yd):
            @step("f" + b + s + s)
            def _():
                wait(b + s + s)
                wsend(b + "q" + s, -d, yd, part["B" + s], xdev[s])

            @step("f" + b + o + s)
            def _():
                wait(b + o + s)
                wsend("S" + b + s, -d, yd, part["B"], sib)

            @step("f" + b + "q" + s)
            def _():
                wait(b + "q" + s)
                wsend("S" + b + "q" + s, -2 * d, yd, part["B" + s], sib)

        a_piece(s)
        a_piece(o)
        b_piece("B", "y")
        b_piece("Bo", "n")

        @step("fAq" + s)
        def _():
            wait("Aq" + s)
            wsend("Ayq" + s, -2 * d, "y", part["A" + s], ydev)
            wsend("SAq" + s, -2 * d, "y", part["A" + s], sib)

        @step("fAyq" + s)
        def _():
            wait("Ayq" + s)
            wsend("SAyq" + s, -2 * d, "n", part["A" + s], sib)

    for s, d in SIGN.items():
        for p in SIGN:
            weight_start("A", p, s)
            weight_start("B", p, s)
        weight_steps(s, d)

    yb = {"o": yh, "p": 1 - yh}

    def feature(r, zd):
        return yb[r] * 8 + ring(z, zd, 8)

    def tp(r, zd, i):
        return tfull.at[feature(r, zd), pl.ds(i * hrow, hrow), :]

    def is_long(i, s):
        return (i == 0) == (s == "+")

    def token_start(i):
        mine = tok_hbm.at[pl.ds(i * hrow, hrow), :]

        @step("iTh%d" % i)
        def _():
            send("Th%d" % i, mine, tp("o", 0, i), yhdev)

        def along(s):
            @step("iT%d%s" % (i, s))
            def _():
                send("To%d0%s" % (i, s), mine, tp("o", 0, i), zdev[s])

        for s in SIGN:
            along(s)

        @step("fTP%d" % i)
        def _():
            wait("Th%d" % i)
            for s in SIGN:
                send("Tp%d0%s" % (i, s), tp("p", 0, i), tp("p", 0, i), zdev[s])

    def token_hop(r, i, h, s, d):
        @step("fT%s%d%d%s" % (r, i, h, s))
        def _():
            wait("T%s%d%d%s" % (r, i, h - 1, s))
            if h < 3 + is_long(i, s):
                src = tp(r, -d * h, i)
                send("T%s%d%d%s" % (r, i, h, s), src, src, zdev[s])

    for i in range(2):
        token_start(i)
        for r in "op":
            for s, d in SIGN.items():
                for h in range(1, 4 + is_long(i, s)):
                    token_hop(r, i, h, s, d)

    def as_rows(parts):
        lane = lax.broadcasted_iota(jnp.int32, (rows, 128), 1)
        tile = jnp.zeros((rows, 128), F32)
        for i, p in enumerate(parts):
            tile = jnp.where(lane == i, p, tile)
        return jnp.transpose(tile)[:8, :]

    def as_columns(parts):
        pad = jnp.zeros((128 - len(parts), rows), F32)
        return jnp.transpose(jnp.concatenate(list(parts) + [pad], axis=0))

    def stat_send(which, name, s):
        send(name, st_ring.at[which, z], st_ring.at[which, z], zdev[s])

    def stat_hop(which, p, h, s, d):
        @step("%sS%d%s" % ("fb"[which], h, s))
        def _():
            wait("%st%d%s" % (p, h - 1, s))
            if h < 3 or (h == 3 and d == 1):
                src = st_ring.at[which, ring(z, -d * h, 8)]
                send("%st%d%s" % (p, h, s), src, src, zdev[s])

    for h in range(1, 5):
        for s, d in SIGN.items():
            if h < 4 or d == 1:
                stat_hop(0, "S", h, s, d)
                stat_hop(1, "R", h, s, d)

    @step("iSt")
    def _():
        loads[0].wait()
        own = own_tok[...].astype(F32)
        mean = jnp.mean(own, axis=-1, keepdims=True)
        dev = own - mean
        st_own[0] = as_rows((mean, jnp.sum(dev * dev, axis=-1, keepdims=True)))
        send("Sth", st_own.at[0], st_peer.at[0], yhdev)

    @step("fSt")
    def _():
        wait("Sth")
        a, b = st_own[0], st_peer[0]
        gap = a[0:1] - b[0:1]
        st_ring[0, z] = jnp.concatenate(
            [
                0.5 * (a[0:1] + b[0:1]),
                a[1:2] + b[1:2] + (0.5 * width) * gap * gap,
                jnp.zeros((6, rows), F32),
            ],
            axis=0,
        )
        for s in SIGN:
            stat_send(0, "St0" + s, s)

    @step("stat")
    def _():
        got = st_ring[0]
        means = got[:, 0:1, :]
        mean = jnp.mean(means, axis=0)
        gap = means - mean[None]
        sq = jnp.sum(got[:, 1:2, :], axis=0) + (2.0 * width) * jnp.sum(gap * gap, axis=0)
        cols[0] = as_columns((mean, lax.rsqrt(sq / (16.0 * width) + EPS)))
        normed[:, rows:, :] = jnp.ones_like(normed[:, rows:, :])
        acc[...] = jnp.zeros_like(acc)

    def norm_block(r, zd):
        @step("n%s%d" % (r, zd))
        def _():
            j = feature(r, zd)
            unit = (tfull[j].astype(F32) - cols[0, :, 0:1]) * cols[0, :, 1:2]
            unit = unit.astype(BF16)
            lanes = pl.ds(pl.multiple_of((j % 2) * width, 128), width)
            normed[j // 2, :rows, lanes] = unit
            normt[j] = jnp.transpose(unit)

    last = (ring(z, 4, 8)) // 2

    def multiply(k):
        acc[...] += mm(normed[k], wfull[k], ((1,), (0,)))

    def product(xd, yd, waits):
        @step("m%d%s" % (xd, yd))
        def _():
            wait(*waits)
            if (xd, yd) == (0, "y"):
                loads[1].wait()
            k = ring(x, xd, 4) * 2 + ys[yd]

            @pl.when(lax.rem(k, 4) != last)
            def _():
                multiply(k)

        @step("l%d%s" % (xd, yd))
        def _():
            k = ring(x, xd, 4) * 2 + ys[yd]

            @pl.when(lax.rem(k, 4) == last)
            def _():
                multiply(k)

    product(0, "y", ("S0y",))
    product(0, "n", ("SBy", "SAy"))
    for s, d in SIGN.items():
        product(-d, "y", ("SA+" + s, "SA-" + s, "SB" + s))
        product(-d, "n", ("SAy+" + s, "SAy-" + s, "SBo" + s))
    product(2, "y", ("SAq+", "SAq-", "SBq+", "SBq-"))
    product(2, "n", ("SAyq+", "SAyq-", "SBoq+", "SBoq-"))

    def head(h):
        @step("att%d" % h)
        def _():
            if h == 0:
                loads[2].wait()
            base = 3 * h * HD
            at = [slice(base + i * HD, base + (i + 1) * HD) for i in range(3)]
            qkv = [acc[:rows, a].astype(BF16) for a in at]
            mine = slice(h * HD, (h + 1) * HD)
            out, dq, dk, dv = one_head(*qkv, og_ref[:, mine])
            att_ref[:, mine] = out.astype(BF16)
            for a, g in zip(at, (dq, dk, dv)):
                dqkv[:, a] = g.astype(BF16)
            if h == 1:
                store(att_ref, att_hbm)

    head(0)
    head(1)

    @step("bSt")
    def _():
        d = dqkv[...].astype(F32)
        st_own[1] = as_rows(
            (
                jnp.sum(d * acc[rows : rows + 1, :], axis=-1, keepdims=True),
                jnp.sum(d * acc[:rows, :], axis=-1, keepdims=True),
            )
        )
        send("Rth", st_own.at[1], st_peer.at[1], yhdev)

    @step("bSh")
    def _():
        wait("Rth")
        st_ring[1, z] = st_own[1] + st_peer[1]
        for s in SIGN:
            stat_send(1, "Rt0" + s, s)

    @step("bstat")
    def _():
        sums = jnp.sum(st_ring[1], axis=0) * (1.0 / (16.0 * width))
        cols[1] = as_columns((sums[0:1], sums[1:2]))

    def bp(r, zd, i):
        return bk.at[feature(r, zd), pl.ds(i * hrow, hrow), :]

    def add(dst, *srcs):
        total = dst[...].astype(F32)
        for src in srcs:
            total = total + src[...].astype(F32)
        dst[...] = total.astype(BF16)

    def back(r, zd):
        @step("c%s%d" % (r, zd))
        def _():
            j = feature(r, zd)
            w = wfull[j // 2, pl.ds(pl.multiple_of((j % 2) * depth, 16), depth), :]
            bk[j] = mm(dqkv[...], w, ((1,), (1,))).astype(BF16)
            if zd == 4:
                back_send(r, 0, 0, "+", 4)
                back_send(r, 1, 0, "-", 4)

    def back_send(r, i, h, s, zd):
        dst = bin.at["op".index(r), i, "+-".index(s), h]
        send("K%s%d%d%s" % (r, i, h, s), bp(r, zd, i), dst, zdev[s])

    def got(r, i, h, s):
        return bin.at["op".index(r), i, "+-".index(s), h]

    def back_hop(r, i, h, s, d):
        @step("k%s%d%d%s" % (r, i, h, s))
        def _():
            zd = d * (4 - h)
            if h > 1 or is_long(i, s):
                wait("K%s%d%d%s" % (r, i, h - 1, s))
                add(bp(r, zd, i), got(r, i, h - 1, s))
            back_send(r, i, h, s, zd)

    for r in "op":
        for zd in (0, 1, 2, 3, 4, -1, -2, -3):
            norm_block(r, zd)
            back(r, zd)
        for i in range(2):
            for h in (1, 2, 3):
                for s, d in SIGN.items():
                    back_hop(r, i, h, s, d)

    def back_end(i):
        mine = pl.ds(i * hrow, hrow)

        @step("kp%d" % i)
        def _():
            wait("Kp%d3+" % i, "Kp%d3-" % i)
            add(bp("p", 0, i), got("p", i, 3, "+"), got("p", i, 3, "-"))
            send("Kh%d" % i, bp("p", 0, i), by.at[mine, :], yhdev)

        @step("ft%d" % i)
        def _():
            wait("Ko%d3+" % i, "Ko%d3-" % i, "Kh%d" % i)
            total = bp("o", 0, i)[...].astype(F32) + by[mine, :].astype(F32)
            for s in SIGN:
                total = total + got("o", i, 3, s)[...].astype(F32)
            mean, inv = cols[0, mine, 0:1], cols[0, mine, 1:2]
            unit = (tp("o", 0, i)[...].astype(F32) - mean) * inv
            gt_ref[mine, :] = inv * (total - cols[1, mine, 0:1] - unit * cols[1, mine, 1:2])
            store(gt_ref.at[mine, :], gt_hbm.at[mine, :])

    back_end(0)
    back_end(1)

    def chip(xd, yd):
        return ring(x, xd, 4) * 2 + ys[yd]

    def gp(xd, yd, rng, lanes=slice(None)):
        return gown.at[chip(xd, yd), pl.ds(*rng), lanes]

    XS = (0, 1, -1, 2)
    TOWARD = {1: "+", -1: "-"}

    def part_name(h):
        return "" if h is None else str(h)

    def grad(xd, yd, h=None):
        lanes = slice(None) if h is None else pl.ds(h * 3 * HD, 3 * HD)
        name = "%d%s%s" % (xd, yd, part_name(h))
        yi = "yn".index(yd)

        def block(ref):
            return ref.at[chip(xd, yd), :, lanes]

        @step("g" + name)
        def _():
            out = block(gout)
            out[...] = mm(normt[2 * chip(xd, yd) + 1 - c], dqkv[:, lanes], ((1,), (0,))).astype(BF16)
            send("G" + name, out, block(gin), sib)

        @step("o" + name)
        def _():
            mine = mm(normt[2 * chip(xd, yd) + c], dqkv[:, lanes], ((1,), (0,)))
            block(gown)[...] = mine.astype(BF16)

        @step("j" + name)
        def _():
            wait("G" + name)
            add(block(gown), block(gin))
            if yd == "n":
                dst = gya.at[XS.index(xd), :, lanes]
                send("Y%d%s" % (xd, part_name(h)), gp(xd, "n", part["A"], lanes), dst, ydev)
            if xd == 2:
                for s in SIGN:
                    dst = gbq[s].at[yi, :, lanes]
                    send("BQ" + yd + s + part_name(h), gp(2, yd, part["B" + s], lanes), dst, xdev[s])
            elif xd != 0:
                s = TOWARD[xd]
                p = OTHER[s]
                send("BF" + yd + s, gp(xd, yd, part["B" + p]), gbf[p].at[yi], xdev[s])

    def sum_y(xd, h=None):
        lanes = slice(None) if h is None else pl.ds(h * 3 * HD, 3 * HD)
        name = "%d%s" % (xd, part_name(h))

        @step("ya" + name)
        def _():
            wait("Y" + name)
            add(gp(xd, "y", part["A"], lanes), gya.at[XS.index(xd), :, lanes])
            if xd == 2:
                for s in SIGN:
                    dst = gaq[s].at[:, lanes]
                    send("AQ" + s + part_name(h), gp(2, "y", part["A" + s], lanes), dst, xdev[s])
            elif xd != 0:
                s = TOWARD[xd]
                p = OTHER[s]
                send("AF" + s, gp(xd, "y", part["A" + p]), gaf[p], xdev[s])

    def sum_x(s, d):
        def along(yd):
            yi = "yn".index(yd)

            @step("bh" + yd + s)
            def _():
                wait("BQ" + yd + s + "0", "BQ" + yd + s + "1")
                add(gp(d, yd, part["B" + s]), gbq[s].at[yi])
                send("BD" + yd + s, gp(d, yd, part["B" + s]), gbd[s].at[yi], xdev[s])

        along("y")
        along("n")

        @step("ah" + s)
        def _():
            wait("AQ" + s + "0", "AQ" + s + "1")
            add(gp(d, "y", part["A" + s]), gaq[s])
            send("AD" + s, gp(d, "y", part["A" + s]), gad[s], xdev[s])

        @step("bn" + s)
        def _():
            wait("BDn" + s, "BFn" + OTHER[s])
            add(gp(0, "n", part["B" + s]), gbd[s].at[1], gbf[s].at[1])
            send("Yb" + s, gp(0, "n", part["B" + s]), gyb[s], ydev)

        def finish(rng, *terms):
            total = gp(0, "y", rng)[...].astype(F32)
            for t in terms:
                total = total + t[...].astype(F32)
            mine = pl.ds(*rng)
            gw_ref[mine, :] = total.astype(BF16)
            store(gw_ref.at[mine, :], gw_hbm.at[mine, :])

        @step("fgA" + s)
        def _():
            wait("AD" + s, "AF" + OTHER[s])
            finish(part["A" + s], gad[s], gaf[s])

        @step("fgB" + s)
        def _():
            wait("BDy" + s, "BFy" + OTHER[s], "Yb" + s)
            finish(part["B" + s], gbd[s].at[0], gbf[s].at[0], gyb[s])

    for xd in XS:
        for h in (0, 1) if xd == 2 else (None,):
            grad(xd, "y", h)
            grad(xd, "n", h)
            sum_y(xd, h)
    for s, d in SIGN.items():
        sum_x(s, d)

    for cp in loads:
        cp.start()
    barrier = pltpu.get_barrier_semaphore()
    everyone = [sib, ydev, xdev["+"], xdev["-"], zdev["+"], zdev["-"], yhdev]
    for dev in everyone:
        pl.semaphore_signal(barrier, inc=1, device_id=dev, device_id_type=MESH)
    pl.semaphore_wait(barrier, len(everyone))

    todo = list(steps.values())
    assert sorted(ORDER) == list(range(len(todo)))
    for n in ORDER:
        todo[n]()
    assert len(copies) == COPIES
    for cp in copies.values():
        cp.wait_send()
    for cp in stores:
        cp.wait()


COPIES = 166


def hand_over(*refs):
    for src, dst in zip(refs[:3], refs[3:]):
        dst[...] = src[...]


def per_device(tokens, w_qkv, out_grad):
    rows, width = tokens.shape
    depth, wide = w_qkv.shape
    part = split_rows(depth)
    vmem = pltpu.VMEM

    def count(name):
        return part[name][1]

    a_part = {s: vmem((count("A" + s), wide), BF16) for s in SIGN}
    b_part = {s: vmem((count("B" + s), wide), BF16) for s in SIGN}
    b_pair = {s: vmem((2, count("B" + s), wide), BF16) for s in SIGN}
    scratch = [
        vmem(out_grad.shape, BF16),
        vmem(out_grad.shape, BF16),
        vmem(tokens.shape, F32),
        vmem(w_qkv.shape, BF16),
        pltpu.SemaphoreType.DMA((3,)),
        pltpu.SemaphoreType.DMA((7,)),
        vmem((8, 2 * depth, wide), BF16),
        vmem((16, rows, width), BF16),
        vmem((8, rows + 16, 2 * width), BF16),
        vmem((16, width, rows), BF16),
        vmem((rows + 16, wide), F32),
        vmem((rows, wide), BF16),
        vmem((2, rows, 128), F32),
        vmem((8, depth, wide), BF16),
        vmem((8, depth, wide), BF16),
        vmem((8, depth, wide), BF16),
        vmem((4, count("A"), wide), BF16),
        a_part, a_part, a_part, b_pair, b_pair, b_pair, b_part,
        vmem((16, rows, width), BF16),
        vmem((2, 2, 2, 4, rows // 2, width), BF16),
        vmem((rows, width), BF16),
        vmem((2, 8, rows), F32),
        vmem((2, 8, rows), F32),
        vmem((2, 8, 8, rows), F32),
        pltpu.SemaphoreType.DMA((COPIES,)),
        pltpu.SemaphoreType.DMA((COPIES,)),
    ]
    anywhere = pl.BlockSpec(memory_space=pl.ANY)
    results = pl.pallas_call(
        kernel,
        out_shape=(
            jax.ShapeDtypeStruct(out_grad.shape, BF16),
            jax.ShapeDtypeStruct(tokens.shape, F32),
            jax.ShapeDtypeStruct(w_qkv.shape, BF16),
        ),
        in_specs=[anywhere] * 3,
        out_specs=(anywhere,) * 3,
        scratch_shapes=scratch,
        compiler_params=pltpu.CompilerParams(
            collective_id=0, has_side_effects=True, vmem_limit_bytes=62 * 1024 * 1024
        ),
    )(tokens, w_qkv, out_grad)
    in_vmem = [pl.BlockSpec(memory_space=vmem)] * 3
    return pl.pallas_call(
        hand_over,
        out_shape=[jax.ShapeDtypeStruct(r.shape, r.dtype) for r in results],
        in_specs=in_vmem,
        out_specs=in_vmem,
    )(*results)


def solution(mesh):
    placed = (P("dp", "mp"), P("dp", "mp"), P("dp", "mp"))
    return jax.shard_map(
        per_device, mesh=mesh, in_specs=placed, out_specs=placed, check_vma=False
    )
```

```python
import jax
import jax.numpy as jnp
from jax import lax
from jax.experimental import pallas as pl
from jax.experimental.pallas import tpu as pltpu
from jax.sharding import PartitionSpec as P

HD = 128
EPS = 1e-06
F32 = jnp.float32
BF16 = jnp.bfloat16
MESH = pl.DeviceIdType.MESH
SIGN = {"+": 1, "-": -1}
OTHER = {"+": "-", "-": "+"}

ORDER = (
    87, 23, 7, 55, 37, 5, 1, 39, 56, 21,
    24, 38, 57, 6, 8, 22, 0, 2, 88, 25,
    11, 45, 59, 58, 62, 27, 75, 9, 73, 40,
    41, 46, 60, 13, 29, 69, 66, 77, 63, 79,
    48, 3, 30, 14, 52, 42, 35, 19, 47, 61,
    4, 70, 67, 81, 31, 15, 26, 64, 83, 49,
    12, 53, 43, 16, 32, 28, 71, 68, 85, 89,
    143, 115, 141, 117, 105, 103, 133, 113, 135, 131,
    33, 17, 50, 145, 10, 107, 65, 109, 36, 54,
    137, 90, 91, 92, 93, 94, 18, 44, 111, 72,
    34, 20, 51, 139, 96, 95, 97, 98, 187, 188,
    99, 191, 178, 140, 189, 195, 194, 146, 148, 104,
    170, 112, 171, 180, 100, 196, 164, 181, 134, 172,
    138, 153, 142, 192, 182, 154, 147, 193, 174, 106,
    167, 132, 173, 177, 116, 101, 184, 136, 166, 118,
    120, 205, 114, 175, 199, 197, 185, 155, 126, 179,
    163, 186, 190, 144, 150, 168, 108, 149, 156, 74,
    76, 110, 119, 125, 165, 183, 122, 157, 128, 151,
    78, 176, 207, 152, 121, 158, 80, 127, 201, 169,
    124, 130, 198, 204, 82, 206, 200, 159, 123, 161,
    84, 129, 86, 102, 203, 209, 160, 202, 208, 162,
)


def mm(a, b, dims):
    return lax.dot_general(a, b, (dims, ((), ())), preferred_element_type=F32)


def normalize(v):
    centred = v - jnp.mean(v, axis=-1, keepdims=True)
    inv = lax.rsqrt(jnp.mean(centred * centred, axis=-1, keepdims=True) + EPS)
    return centred * inv, inv


def normalize_back(d, unit, inv):
    return inv * (
        d
        - jnp.mean(d, axis=-1, keepdims=True)
        - unit * jnp.mean(d * unit, axis=-1, keepdims=True)
    )


def split(v, which):
    high = v.astype(BF16)
    low = (v - high.astype(F32)).astype(BF16)
    return jnp.concatenate((high, high, low) if which else (high, low, high), axis=1)


def one_head(q, k, v, og):
    qu, qi = normalize(q.astype(F32))
    ku, ki = normalize(k.astype(F32))
    scale = 1.0 / (HD**0.5)
    scores = mm(split(qu, 0), split(ku, 1), ((1,), (1,))) * scale
    weights = jnp.exp(scores)
    probs = weights / jnp.sum(weights, axis=-1, keepdims=True)
    probs16 = probs.astype(BF16)
    out = mm(probs16, v, ((1,), (0,)))
    dv = mm(probs16, og, ((0,), (0,)))
    dp = mm(og, v, ((1,), (1,)))
    ds = (probs * (dp - jnp.sum(dp * probs, axis=-1, keepdims=True)) * scale).astype(BF16)
    dq = normalize_back(mm(ds, ku.astype(BF16), ((1,), (0,))), qu, qi)
    dk = normalize_back(mm(ds, qu.astype(BF16), ((0,), (0,))), ku, ki)
    return out, dq, dk, dv


def split_rows(depth):
    a = depth // 3
    ap = depth // 6
    bp = depth // 3
    return {
        "A": (0, a),
        "B": (a, depth - a),
        "A+": (0, ap),
        "A-": (ap, a - ap),
        "B+": (a, bp),
        "B-": (a + bp, depth - a - bp),
    }


def kernel(
    tok_hbm, w_hbm, og_hbm,
    att_hbm, gt_hbm, gw_hbm,
    og_ref, att_ref, gt_ref, gw_ref, load_sem, store_sem,
    wfull, tfull, normed, normt, acc, dqkv, cols,
    gown, gout, gin, gya, gaq, gaf, gad, gbq, gbf, gbd, gyb,
    bk, bin, by, st_own, st_peer, st_ring,
    send_sem, recv_sem,
):
    dp, mp = lax.axis_index("dp"), lax.axis_index("mp")
    x, y, c = dp // 4, (dp // 2) % 2, dp % 2
    yh, z = mp // 8, mp % 8
    rows, width = tok_hbm.shape
    depth = w_hbm.shape[0]
    hrow = rows // 2
    part = split_rows(depth)

    def ring(v, d, n):
        return lax.rem(v + d + n, n)

    sib = {"dp": dp + 1 - 2 * c}
    ydev = {"dp": x * 4 + (1 - y) * 2 + c}
    xdev = {s: {"dp": ring(x, d, 4) * 4 + y * 2 + c} for s, d in SIGN.items()}
    zdev = {s: {"mp": yh * 8 + ring(z, d, 8)} for s, d in SIGN.items()}
    yhdev = {"mp": (1 - yh) * 8 + z}

    own_tok = tfull.at[mp]
    own_w = wfull.at[x * 2 + y, pl.ds(pl.multiple_of(c * depth, 16), depth), :]
    loads = [
        pltpu.make_async_copy(src, dst, load_sem.at[i])
        for i, (src, dst) in enumerate(((tok_hbm, own_tok), (w_hbm, own_w), (og_hbm, og_ref)))
    ]
    stores = []

    def store(src, dst):
        cp = pltpu.make_async_copy(src, dst, store_sem.at[len(stores)])
        cp.start()
        stores.append(cp)

    copies = {}
    steps = {}

    def send(name, src, dst, dev):
        n = len(copies)
        cp = pltpu.make_async_remote_copy(
            src_ref=src, dst_ref=dst, send_sem=send_sem.at[n], recv_sem=recv_sem.at[n],
            device_id=dev, device_id_type=MESH,
        )
        cp.start()
        copies[name] = cp

    def wait(*names):
        for name in names:
            copies[name].wait_recv()

    def step(name):
        def keep(f):
            steps[name] = f
        return keep

    ys = {"y": y, "n": 1 - y}

    def wp(xd, yd, rng):
        r = pl.multiple_of(c * depth + rng[0], 16)
        return wfull.at[ring(x, xd, 4) * 2 + ys[yd], pl.ds(r, rng[1]), :]

    def wown(name, rng, dev):
        send(name, w_hbm.at[pl.ds(*rng), :], wp(0, "y", rng), dev)

    def wsend(name, xd, yd, rng, dev):
        send(name, wp(xd, yd, rng), wp(xd, yd, rng), dev)

    @step("iS")
    def _():
        wown("S0y", (0, depth), sib)

    @step("iBy")
    def _():
        wown("By", part["B"], ydev)

    @step("iAy")
    def _():
        wown("Ay", part["A"], ydev)

    @step("fBy")
    def _():
        wait("By")
        for p, s in (("+", "+"), ("-", "-"), ("-", "+"), ("+", "-")):
            wsend("Bo" + p + s, 0, "n", part["B" + p], xdev[s])
        wsend("SBy", 0, "n", part["B"], sib)

    @step("fAy")
    def _():
        wait("Ay")
        wsend("SAy", 0, "n", part["A"], sib)

    def weight_start(k, p, s):
        @step("i" + k + p + s)
        def _():
            wown(k + p + s, part[k + p], xdev[s])

    def weight_steps(s, d):
        o = OTHER[s]

        def a_piece(p):
            @step("fA" + p + s)
            def _():
                wait("A" + p + s)
                if p == s:
                    wsend("Aq" + s, -d, "y", part["A" + s], xdev[s])
                wsend("Ay" + p + s, -d, "y", part["A" + p], ydev)
                wsend("SA" + p + s, -d, "y", part["A" + p], sib)

            @step("fAy" + p + s)
            def _():
                wait("Ay" + p + s)
                wsend("SAy" + p + s, -d, "n", part["A" + p], sib)

        def b_piece(b, yd):
            @step("f" + b + s + s)
            def _():
                wait(b + s + s)
                wsend(b + "q" + s, -d, yd, part["B" + s], xdev[s])

            @step("f" + b + o + s)
            def _():
                wait(b + o + s)
                wsend("S" + b + s, -d, yd, part["B"], sib)

            @step("f" + b + "q" + s)
            def _():
                wait(b + "q" + s)
                wsend("S" + b + "q" + s, -2 * d, yd, part["B" + s], sib)

        a_piece(s)
        a_piece(o)
        b_piece("B", "y")
        b_piece("Bo", "n")

        @step("fAq" + s)
        def _():
            wait("Aq" + s)
            wsend("Ayq" + s, -2 * d, "y", part["A" + s], ydev)
            wsend("SAq" + s, -2 * d, "y", part["A" + s], sib)

        @step("fAyq" + s)
        def _():
            wait("Ayq" + s)
            wsend("SAyq" + s, -2 * d, "n", part["A" + s], sib)

    for s, d in SIGN.items():
        for p in SIGN:
            weight_start("A", p, s)
            weight_start("B", p, s)
        weight_steps(s, d)

    yb = {"o": yh, "p": 1 - yh}

    def feature(r, zd):
        return yb[r] * 8 + ring(z, zd, 8)

    def tp(r, zd, i):
        return tfull.at[feature(r, zd), pl.ds(i * hrow, hrow), :]

    def is_long(i, s):
        return (i == 0) == (s == "+")

    def token_start(i):
        mine = tok_hbm.at[pl.ds(i * hrow, hrow), :]

        @step("iTh%d" % i)
        def _():
            send("Th%d" % i, mine, tp("o", 0, i), yhdev)

        def along(s):
            @step("iT%d%s" % (i, s))
            def _():
                send("To%d0%s" % (i, s), mine, tp("o", 0, i), zdev[s])

        for s in SIGN:
            along(s)

        @step("fTP%d" % i)
        def _():
            wait("Th%d" % i)
            for s in SIGN:
                send("Tp%d0%s" % (i, s), tp("p", 0, i), tp("p", 0, i), zdev[s])

    def token_hop(r, i, h, s, d):
        @step("fT%s%d%d%s" % (r, i, h, s))
        def _():
            wait("T%s%d%d%s" % (r, i, h - 1, s))
            if h < 3 + is_long(i, s):
                src = tp(r, -d * h, i)
                send("T%s%d%d%s" % (r, i, h, s), src, src, zdev[s])

    for i in range(2):
        token_start(i)
        for r in "op":
            for s, d in SIGN.items():
                for h in range(1, 4 + is_long(i, s)):
                    token_hop(r, i, h, s, d)

    def as_rows(parts):
        lane = lax.broadcasted_iota(jnp.int32, (rows, 128), 1)
        tile = jnp.zeros((rows, 128), F32)
        for i, p in enumerate(parts):
            tile = jnp.where(lane == i, p, tile)
        return jnp.transpose(tile)[:8, :]

    def as_columns(parts):
        pad = jnp.zeros((128 - len(parts), rows), F32)
        return jnp.transpose(jnp.concatenate(list(parts) + [pad], axis=0))

    def stat_send(which, name, s):
        send(name, st_ring.at[which, z], st_ring.at[which, z], zdev[s])

    def stat_hop(which, p, h, s, d):
        @step("%sS%d%s" % ("fb"[which], h, s))
        def _():
            wait("%st%d%s" % (p, h - 1, s))
            if h < 3 or (h == 3 and d == 1):
                src = st_ring.at[which, ring(z, -d * h, 8)]
                send("%st%d%s" % (p, h, s), src, src, zdev[s])

    for h in range(1, 5):
        for s, d in SIGN.items():
            if h < 4 or d == 1:
                stat_hop(0, "S", h, s, d)
                stat_hop(1, "R", h, s, d)

    @step("iSt")
    def _():
        loads[0].wait()
        own = own_tok[...].astype(F32)
        mean = jnp.mean(own, axis=-1, keepdims=True)
        dev = own - mean
        st_own[0] = as_rows((mean, jnp.sum(dev * dev, axis=-1, keepdims=True)))
        send("Sth", st_own.at[0], st_peer.at[0], yhdev)

    @step("fSt")
    def _():
        wait("Sth")
        a, b = st_own[0], st_peer[0]
        gap = a[0:1] - b[0:1]
        st_ring[0, z] = jnp.concatenate(
            [
                0.5 * (a[0:1] + b[0:1]),
                a[1:2] + b[1:2] + (0.5 * width) * gap * gap,
                jnp.zeros((6, rows), F32),
            ],
            axis=0,
        )
        for s in SIGN:
            stat_send(0, "St0" + s, s)

    @step("stat")
    def _():
        got = st_ring[0]
        means = got[:, 0:1, :]
        mean = jnp.mean(means, axis=0)
        gap = means - mean[None]
        sq = jnp.sum(got[:, 1:2, :], axis=0) + (2.0 * width) * jnp.sum(gap * gap, axis=0)
        cols[0] = as_columns((mean, lax.rsqrt(sq / (16.0 * width) + EPS)))
        normed[:, rows:, :] = jnp.ones_like(normed[:, rows:, :])
        acc[...] = jnp.zeros_like(acc)

    def norm_block(r, zd):
        @step("n%s%d" % (r, zd))
        def _():
            j = feature(r, zd)
            unit = (tfull[j].astype(F32) - cols[0, :, 0:1]) * cols[0, :, 1:2]
            unit = unit.astype(BF16)
            lanes = pl.ds(pl.multiple_of((j % 2) * width, 128), width)
            normed[j // 2, :rows, lanes] = unit
            normt[j] = jnp.transpose(unit)

    far = ring(z, 4, 8) // 2
    same_x, same_y = far // 2 == lax.rem(x, 2), lax.rem(far, 2) == y

    def pick(*four):
        a, b, c_, d_ = [ring(x, xd, 4) * 2 + ys[yd] for xd, yd in four]
        return jnp.where(same_y, jnp.where(same_x, a, b), jnp.where(same_x, c_, d_))

    def product(name, k, *chips):
        @step(name)
        def _():
            for chip_name in chips:
                wait(*arrivals[chip_name])
                if chip_name == (0, "y"):
                    loads[1].wait()
            acc[...] += mm(normed[k], wfull[k], ((1,), (0,)))

    arrivals = {
        (0, "y"): ("S0y",),
        (0, "n"): ("SBy", "SAy"),
        (2, "y"): ("SAq+", "SAq-", "SBq+", "SBq-"),
        (2, "n"): ("SAyq+", "SAyq-", "SBoq+", "SBoq-"),
    }
    for s, d in SIGN.items():
        arrivals[-d, "y"] = ("SA+" + s, "SA-" + s, "SB" + s)
        arrivals[-d, "n"] = ("SAy+" + s, "SAy-" + s, "SBo" + s)
    y0, y1, y9, y2 = (0, "y"), (1, "y"), (-1, "y"), (2, "y")
    n0, n1, n9, n2 = (0, "n"), (1, "n"), (-1, "n"), (2, "n")
    product("m0", pick(y1, y0, y0, y0), y0, y1)
    product("m1", pick(y9, y2, y1, y1), y9, y2)
    product("m2", pick(n0, n0, y9, y9), n0)
    product("m3", pick(n1, n1, y2, y2), n1)
    product("m4", pick(n9, n9, n1, n0), n9)
    product("m5", pick(y0, y1, n0, n1))
    product("m6", pick(y2, y9, n9, n9))
    product("m7", pick(n2, n2, n2, n2), n2)

    def head(h):
        @step("att%d" % h)
        def _():
            if h == 0:
                loads[2].wait()
            base = 3 * h * HD
            at = [slice(base + i * HD, base + (i + 1) * HD) for i in range(3)]
            qkv = [acc[:rows, a].astype(BF16) for a in at]
            mine = slice(h * HD, (h + 1) * HD)
            out, dq, dk, dv = one_head(*qkv, og_ref[:, mine])
            att_ref[:, mine] = out.astype(BF16)
            for a, g in zip(at, (dq, dk, dv)):
                dqkv[:, a] = g.astype(BF16)
            if h == 1:
                store(att_ref, att_hbm)

    head(0)
    head(1)

    @step("bSt")
    def _():
        d = dqkv[...].astype(F32)
        st_own[1] = as_rows(
            (
                jnp.sum(d * acc[rows : rows + 1, :], axis=-1, keepdims=True),
                jnp.sum(d * acc[:rows, :], axis=-1, keepdims=True),
            )
        )
        send("Rth", st_own.at[1], st_peer.at[1], yhdev)

    @step("bSh")
    def _():
        wait("Rth")
        st_ring[1, z] = st_own[1] + st_peer[1]
        for s in SIGN:
            stat_send(1, "Rt0" + s, s)

    @step("bstat")
    def _():
        sums = jnp.sum(st_ring[1], axis=0) * (1.0 / (16.0 * width))
        cols[1] = as_columns((sums[0:1], sums[1:2]))

    def bp(r, zd, i):
        return bk.at[feature(r, zd), pl.ds(i * hrow, hrow), :]

    def add(dst, *srcs):
        total = dst[...].astype(F32)
        for src in srcs:
            total = total + src[...].astype(F32)
        dst[...] = total.astype(BF16)

    def back(r, zd):
        @step("c%s%d" % (r, zd))
        def _():
            j = feature(r, zd)
            w = wfull[j // 2, pl.ds(pl.multiple_of((j % 2) * depth, 16), depth), :]
            bk[j] = mm(dqkv[...], w, ((1,), (1,))).astype(BF16)
            if zd == 4:
                back_send(r, 0, 0, "+", 4)
                back_send(r, 1, 0, "-", 4)

    def back_send(r, i, h, s, zd):
        dst = bin.at["op".index(r), i, "+-".index(s), h]
        send("K%s%d%d%s" % (r, i, h, s), bp(r, zd, i), dst, zdev[s])

    def got(r, i, h, s):
        return bin.at["op".index(r), i, "+-".index(s), h]

    def back_hop(r, i, h, s, d):
        @step("k%s%d%d%s" % (r, i, h, s))
        def _():
            zd = d * (4 - h)
            if h > 1 or is_long(i, s):
                wait("K%s%d%d%s" % (r, i, h - 1, s))
                add(bp(r, zd, i), got(r, i, h - 1, s))
            back_send(r, i, h, s, zd)

    for r in "op":
        for zd in (0, 1, 2, 3, 4, -1, -2, -3):
            norm_block(r, zd)
            back(r, zd)
        for i in range(2):
            for h in (1, 2, 3):
                for s, d in SIGN.items():
                    back_hop(r, i, h, s, d)

    def back_end(i):
        mine = pl.ds(i * hrow, hrow)

        @step("kp%d" % i)
        def _():
            wait("Kp%d3+" % i, "Kp%d3-" % i)
            add(bp("p", 0, i), got("p", i, 3, "+"), got("p", i, 3, "-"))
            send("Kh%d" % i, bp("p", 0, i), by.at[mine, :], yhdev)

        @step("ft%d" % i)
        def _():
            wait("Ko%d3+" % i, "Ko%d3-" % i, "Kh%d" % i)
            total = bp("o", 0, i)[...].astype(F32) + by[mine, :].astype(F32)
            for s in SIGN:
                total = total + got("o", i, 3, s)[...].astype(F32)
            mean, inv = cols[0, mine, 0:1], cols[0, mine, 1:2]
            unit = (tp("o", 0, i)[...].astype(F32) - mean) * inv
            gt_ref[mine, :] = inv * (total - cols[1, mine, 0:1] - unit * cols[1, mine, 1:2])
            store(gt_ref.at[mine, :], gt_hbm.at[mine, :])

    back_end(0)
    back_end(1)

    def chip(xd, yd):
        return ring(x, xd, 4) * 2 + ys[yd]

    def gp(xd, yd, rng, lanes=slice(None)):
        return gown.at[chip(xd, yd), pl.ds(*rng), lanes]

    XS = (0, 1, -1, 2)
    TOWARD = {1: "+", -1: "-"}

    def part_name(h):
        return "" if h is None else str(h)

    def grad(xd, yd, h=None):
        lanes = slice(None) if h is None else pl.ds(h * 3 * HD, 3 * HD)
        name = "%d%s%s" % (xd, yd, part_name(h))
        yi = "yn".index(yd)

        def block(ref):
            return ref.at[chip(xd, yd), :, lanes]

        @step("g" + name)
        def _():
            out = block(gout)
            out[...] = mm(normt[2 * chip(xd, yd) + 1 - c], dqkv[:, lanes], ((1,), (0,))).astype(BF16)
            send("G" + name, out, block(gin), sib)

        @step("o" + name)
        def _():
            mine = mm(normt[2 * chip(xd, yd) + c], dqkv[:, lanes], ((1,), (0,)))
            block(gown)[...] = mine.astype(BF16)

        @step("j" + name)
        def _():
            wait("G" + name)
            add(block(gown), block(gin))
            if yd == "n":
                dst = gya.at[XS.index(xd), :, lanes]
                send("Y%d%s" % (xd, part_name(h)), gp(xd, "n", part["A"], lanes), dst, ydev)
            if xd == 2:
                for s in SIGN:
                    dst = gbq[s].at[yi, :, lanes]
                    send("BQ" + yd + s + part_name(h), gp(2, yd, part["B" + s], lanes), dst, xdev[s])
            elif xd != 0:
                s = TOWARD[xd]
                p = OTHER[s]
                send("BF" + yd + s, gp(xd, yd, part["B" + p]), gbf[p].at[yi], xdev[s])

    def sum_y(xd, h=None):
        lanes = slice(None) if h is None else pl.ds(h * 3 * HD, 3 * HD)
        name = "%d%s" % (xd, part_name(h))

        @step("ya" + name)
        def _():
            wait("Y" + name)
            add(gp(xd, "y", part["A"], lanes), gya.at[XS.index(xd), :, lanes])
            if xd == 2:
                for s in SIGN:
                    dst = gaq[s].at[:, lanes]
                    send("AQ" + s + part_name(h), gp(2, "y", part["A" + s], lanes), dst, xdev[s])
            elif xd != 0:
                s = TOWARD[xd]
                p = OTHER[s]
                send("AF" + s, gp(xd, "y", part["A" + p]), gaf[p], xdev[s])

    def sum_x(s, d):
        def along(yd):
            yi = "yn".index(yd)

            @step("bh" + yd + s)
            def _():
                wait("BQ" + yd + s + "0", "BQ" + yd + s + "1")
                add(gp(d, yd, part["B" + s]), gbq[s].at[yi])
                send("BD" + yd + s, gp(d, yd, part["B" + s]), gbd[s].at[yi], xdev[s])

        along("y")
        along("n")

        @step("ah" + s)
        def _():
            wait("AQ" + s + "0", "AQ" + s + "1")
            add(gp(d, "y", part["A" + s]), gaq[s])
            send("AD" + s, gp(d, "y", part["A" + s]), gad[s], xdev[s])

        @step("bn" + s)
        def _():
            wait("BDn" + s, "BFn" + OTHER[s])
            add(gp(0, "n", part["B" + s]), gbd[s].at[1], gbf[s].at[1])
            send("Yb" + s, gp(0, "n", part["B" + s]), gyb[s], ydev)

        def finish(rng, *terms):
            total = gp(0, "y", rng)[...].astype(F32)
            for t in terms:
                total = total + t[...].astype(F32)
            mine = pl.ds(*rng)
            gw_ref[mine, :] = total.astype(BF16)
            store(gw_ref.at[mine, :], gw_hbm.at[mine, :])

        @step("fgA" + s)
        def _():
            wait("AD" + s, "AF" + OTHER[s])
            finish(part["A" + s], gad[s], gaf[s])

        @step("fgB" + s)
        def _():
            wait("BDy" + s, "BFy" + OTHER[s], "Yb" + s)
            finish(part["B" + s], gbd[s].at[0], gbf[s].at[0], gyb[s])

    for xd in XS:
        for h in (0, 1) if xd == 2 else (None,):
            grad(xd, "y", h)
            grad(xd, "n", h)
            sum_y(xd, h)
    for s, d in SIGN.items():
        sum_x(s, d)

    for cp in loads:
        cp.start()
    barrier = pltpu.get_barrier_semaphore()
    everyone = [sib, ydev, xdev["+"], xdev["-"], zdev["+"], zdev["-"], yhdev]
    for dev in everyone:
        pl.semaphore_signal(barrier, inc=1, device_id=dev, device_id_type=MESH)
    pl.semaphore_wait(barrier, len(everyone))

    todo = list(steps.values())
    assert sorted(ORDER) == list(range(len(todo)))
    for n in ORDER:
        todo[n]()
    assert len(copies) == COPIES
    for cp in copies.values():
        cp.wait_send()
    for cp in stores:
        cp.wait()


COPIES = 166


def hand_over(*refs):
    src, dst, held, sem = refs[:3], refs[3:6], refs[6:9], refs[9]
    order = (2, 1, 0)
    loads = [pltpu.make_async_copy(src[i], held[i], sem.at[0, i]) for i in order]
    stores = [pltpu.make_async_copy(held[i], dst[i], sem.at[1, i]) for i in order]
    for cp in loads:
        cp.start()
    for load, cp in zip(loads, stores):
        load.wait()
        cp.start()
    for cp in stores:
        cp.wait()


def per_device(tokens, w_qkv, out_grad):
    rows, width = tokens.shape
    depth, wide = w_qkv.shape
    part = split_rows(depth)
    vmem = pltpu.VMEM

    def count(name):
        return part[name][1]

    a_part = {s: vmem((count("A" + s), wide), BF16) for s in SIGN}
    b_part = {s: vmem((count("B" + s), wide), BF16) for s in SIGN}
    b_pair = {s: vmem((2, count("B" + s), wide), BF16) for s in SIGN}
    scratch = [
        vmem(out_grad.shape, BF16),
        vmem(out_grad.shape, BF16),
        vmem(tokens.shape, F32),
        vmem(w_qkv.shape, BF16),
        pltpu.SemaphoreType.DMA((3,)),
        pltpu.SemaphoreType.DMA((7,)),
        vmem((8, 2 * depth, wide), BF16),
        vmem((16, rows, width), BF16),
        vmem((8, rows + 16, 2 * width), BF16),
        vmem((16, width, rows), BF16),
        vmem((rows + 16, wide), F32),
        vmem((rows, wide), BF16),
        vmem((2, rows, 128), F32),
        vmem((8, depth, wide), BF16),
        vmem((8, depth, wide), BF16),
        vmem((8, depth, wide), BF16),
        vmem((4, count("A"), wide), BF16),
        a_part, a_part, a_part, b_pair, b_pair, b_pair, b_part,
        vmem((16, rows, width), BF16),
        vmem((2, 2, 2, 4, rows // 2, width), BF16),
        vmem((rows, width), BF16),
        vmem((2, 8, rows), F32),
        vmem((2, 8, rows), F32),
        vmem((2, 8, 8, rows), F32),
        pltpu.SemaphoreType.DMA((COPIES,)),
        pltpu.SemaphoreType.DMA((COPIES,)),
    ]
    anywhere = pl.BlockSpec(memory_space=pl.ANY)
    results = pl.pallas_call(
        kernel,
        out_shape=(
            jax.ShapeDtypeStruct(out_grad.shape, BF16),
            jax.ShapeDtypeStruct(tokens.shape, F32),
            jax.ShapeDtypeStruct(w_qkv.shape, BF16),
        ),
        in_specs=[anywhere] * 3,
        out_specs=(anywhere,) * 3,
        scratch_shapes=scratch,
        compiler_params=pltpu.CompilerParams(
            collective_id=0, has_side_effects=True, vmem_limit_bytes=62 * 1024 * 1024
        ),
    )(tokens, w_qkv, out_grad)
    return pl.pallas_call(
        hand_over,
        out_shape=[jax.ShapeDtypeStruct(r.shape, r.dtype) for r in results],
        in_specs=[pl.BlockSpec(memory_space=pltpu.HBM)] * 3,
        out_specs=[pl.BlockSpec(memory_space=pltpu.HBM)] * 3,
        scratch_shapes=[vmem(r.shape, r.dtype) for r in results]
        + [pltpu.SemaphoreType.DMA((2, 3))],
    )(*results)


def solution(mesh):
    placed = (P("dp", "mp"), P("dp", "mp"), P("dp", "mp"))
    return jax.shard_map(
        per_device, mesh=mesh, in_specs=placed, out_specs=placed, check_vma=False
    )
```

```python
import jax
import jax.numpy as jnp
from jax import lax
from jax.experimental import pallas as pl
from jax.experimental.pallas import tpu as pltpu
from jax.sharding import PartitionSpec as P

HD = 128
EPS = 1e-06
F32 = jnp.float32
BF16 = jnp.bfloat16
MESH = pl.DeviceIdType.MESH
SIGN = {"+": 1, "-": -1}
OTHER = {"+": "-", "-": "+"}

ORDER = (
    39, 87, 24, 37, 56, 23, 8, 55, 38, 0,
    21, 22, 57, 1, 2, 6, 5, 7, 88, 45,
    59, 40, 62, 75, 29, 41, 73, 58, 46, 25,
    60, 52, 27, 13, 48, 14, 63, 79, 9, 42,
    77, 30, 69, 3, 11, 66, 47, 61, 31, 4,
    53, 15, 49, 35, 26, 64, 19, 83, 43, 81,
    28, 70, 67, 32, 10, 16, 54, 50, 12, 65,
    44, 85, 89, 103, 135, 117, 107, 115, 36, 17,
    71, 137, 33, 113, 105, 143, 68, 145, 131, 109,
    111, 133, 141, 90, 91, 20, 92, 93, 94, 34,
    51, 18, 72, 139, 95, 96, 97, 98, 187, 188,
    99, 140, 192, 189, 194, 146, 112, 191, 173, 136,
    163, 180, 195, 196, 104, 193, 118, 142, 148, 138,
    153, 100, 114, 110, 154, 147, 125, 120, 174, 175,
    171, 181, 182, 178, 134, 164, 165, 126, 184, 199,
    197, 177, 108, 116, 101, 205, 119, 155, 166, 132,
    106, 185, 186, 190, 179, 167, 170, 144, 168, 149,
    156, 150, 172, 176, 122, 74, 127, 128, 121, 76,
    183, 157, 158, 201, 207, 151, 152, 78, 169, 198,
    204, 124, 129, 200, 206, 130, 123, 80, 161, 159,
    82, 203, 209, 84, 86, 102, 162, 160, 202, 208,
)


def mm(a, b, dims):
    return lax.dot_general(a, b, (dims, ((), ())), preferred_element_type=F32)


def normalize(v):
    centred = v - jnp.mean(v, axis=-1, keepdims=True)
    inv = lax.rsqrt(jnp.mean(centred * centred, axis=-1, keepdims=True) + EPS)
    return centred * inv, inv


def normalize_back(d, unit, inv):
    return inv * (
        d
        - jnp.mean(d, axis=-1, keepdims=True)
        - unit * jnp.mean(d * unit, axis=-1, keepdims=True)
    )


def split(v, which):
    high = v.astype(BF16)
    low = (v - high.astype(F32)).astype(BF16)
    return jnp.concatenate((high, high, low) if which else (high, low, high), axis=1)


def one_head(q, k, v, og):
    qu, qi = normalize(q.astype(F32))
    ku, ki = normalize(k.astype(F32))
    scale = 1.0 / (HD**0.5)
    scores = mm(split(qu, 0), split(ku, 1), ((1,), (1,))) * scale
    weights = jnp.exp(scores)
    probs = weights / jnp.sum(weights, axis=-1, keepdims=True)
    probs16 = probs.astype(BF16)
    out = mm(probs16, v, ((1,), (0,)))
    dv = mm(probs16, og, ((0,), (0,)))
    dp = mm(og, v, ((1,), (1,)))
    ds = (probs * (dp - jnp.sum(dp * probs, axis=-1, keepdims=True)) * scale).astype(BF16)
    dq = normalize_back(mm(ds, ku.astype(BF16), ((1,), (0,))), qu, qi)
    dk = normalize_back(mm(ds, qu.astype(BF16), ((0,), (0,))), ku, ki)
    return out, dq, dk, dv


def split_rows(depth):
    a = depth // 3
    ap = depth // 6
    bp = depth // 3
    return {
        "A": (0, a),
        "B": (a, depth - a),
        "A+": (0, ap),
        "A-": (ap, a - ap),
        "B+": (a, bp),
        "B-": (a + bp, depth - a - bp),
    }


def kernel(
    tok_hbm, w_hbm, og_hbm,
    att_hbm, gt_hbm, gw_hbm,
    og_ref, att_ref, gt_ref, gw_ref, load_sem, store_sem,
    wfull, tfull, normed, normt, acc, dqkv, cols,
    gown, gout, gin, gya, gaq, gaf, gad, gbq, gbf, gbd, gyb,
    bk, bin, by, st_own, st_peer, st_ring,
    send_sem, recv_sem,
):
    dp, mp = lax.axis_index("dp"), lax.axis_index("mp")
    x, y, c = dp // 4, (dp // 2) % 2, dp % 2
    yh, z = mp // 8, mp % 8
    rows, width = tok_hbm.shape
    depth = w_hbm.shape[0]
    hrow = rows // 2
    part = split_rows(depth)

    def ring(v, d, n):
        return lax.rem(v + d + n, n)

    sib = {"dp": dp + 1 - 2 * c}
    ydev = {"dp": x * 4 + (1 - y) * 2 + c}
    xdev = {s: {"dp": ring(x, d, 4) * 4 + y * 2 + c} for s, d in SIGN.items()}
    zdev = {s: {"mp": yh * 8 + ring(z, d, 8)} for s, d in SIGN.items()}
    yhdev = {"mp": (1 - yh) * 8 + z}

    own_tok = tfull.at[mp]
    own_w = wfull.at[x * 2 + y, pl.ds(pl.multiple_of(c * depth, 16), depth), :]
    loads = [
        pltpu.make_async_copy(src, dst, load_sem.at[i])
        for i, (src, dst) in enumerate(((tok_hbm, own_tok), (w_hbm, own_w), (og_hbm, og_ref)))
    ]
    stores = []

    def store(src, dst):
        cp = pltpu.make_async_copy(src, dst, store_sem.at[len(stores)])
        cp.start()
        stores.append(cp)

    copies = {}
    steps = {}

    def send(name, src, dst, dev):
        n = len(copies)
        cp = pltpu.make_async_remote_copy(
            src_ref=src, dst_ref=dst, send_sem=send_sem.at[n], recv_sem=recv_sem.at[n],
            device_id=dev, device_id_type=MESH,
        )
        cp.start()
        copies[name] = cp

    def wait(*names):
        for name in names:
            copies[name].wait_recv()

    def step(name):
        def keep(f):
            steps[name] = f
        return keep

    ys = {"y": y, "n": 1 - y}

    def wp(xd, yd, rng):
        r = pl.multiple_of(c * depth + rng[0], 16)
        return wfull.at[ring(x, xd, 4) * 2 + ys[yd], pl.ds(r, rng[1]), :]

    def wown(name, rng, dev):
        send(name, w_hbm.at[pl.ds(*rng), :], wp(0, "y", rng), dev)

    def wsend(name, xd, yd, rng, dev):
        send(name, wp(xd, yd, rng), wp(xd, yd, rng), dev)

    @step("iS")
    def _():
        wown("S0y", (0, depth), sib)

    @step("iBy")
    def _():
        wown("By", part["B"], ydev)

    @step("iAy")
    def _():
        wown("Ay", part["A"], ydev)

    @step("fBy")
    def _():
        wait("By")
        for p, s in (("+", "+"), ("-", "-"), ("-", "+"), ("+", "-")):
            wsend("Bo" + p + s, 0, "n", part["B" + p], xdev[s])
        wsend("SBy", 0, "n", part["B"], sib)

    @step("fAy")
    def _():
        wait("Ay")
        wsend("SAy", 0, "n", part["A"], sib)

    def weight_start(k, p, s):
        @step("i" + k + p + s)
        def _():
            wown(k + p + s, part[k + p], xdev[s])

    def weight_steps(s, d):
        o = OTHER[s]

        def a_piece(p):
            @step("fA" + p + s)
            def _():
                wait("A" + p + s)
                if p == s:
                    wsend("Aq" + s, -d, "y", part["A" + s], xdev[s])
                wsend("Ay" + p + s, -d, "y", part["A" + p], ydev)
                wsend("SA" + p + s, -d, "y", part["A" + p], sib)

            @step("fAy" + p + s)
            def _():
                wait("Ay" + p + s)
                wsend("SAy" + p + s, -d, "n", part["A" + p], sib)

        def b_piece(b, yd):
            @step("f" + b + s + s)
            def _():
                wait(b + s + s)
                wsend(b + "q" + s, -d, yd, part["B" + s], xdev[s])

            @step("f" + b + o + s)
            def _():
                wait(b + o + s)
                wsend("S" + b + s, -d, yd, part["B"], sib)

            @step("f" + b + "q" + s)
            def _():
                wait(b + "q" + s)
                wsend("S" + b + "q" + s, -2 * d, yd, part["B" + s], sib)

        a_piece(s)
        a_piece(o)
        b_piece("B", "y")
        b_piece("Bo", "n")

        @step("fAq" + s)
        def _():
            wait("Aq" + s)
            wsend("Ayq" + s, -2 * d, "y", part["A" + s], ydev)
            wsend("SAq" + s, -2 * d, "y", part["A" + s], sib)

        @step("fAyq" + s)
        def _():
            wait("Ayq" + s)
            wsend("SAyq" + s, -2 * d, "n", part["A" + s], sib)

    for s, d in SIGN.items():
        for p in SIGN:
            weight_start("A", p, s)
            weight_start("B", p, s)
        weight_steps(s, d)

    yb = {"o": yh, "p": 1 - yh}

    def feature(r, zd):
        return yb[r] * 8 + ring(z, zd, 8)

    def tp(r, zd, i):
        return tfull.at[feature(r, zd), pl.ds(i * hrow, hrow), :]

    def is_long(i, s):
        return (i == 0) == (s == "+")

    def token_start(i):
        mine = tok_hbm.at[pl.ds(i * hrow, hrow), :]

        @step("iTh%d" % i)
        def _():
            send("Th%d" % i, mine, tp("o", 0, i), yhdev)

        def along(s):
            @step("iT%d%s" % (i, s))
            def _():
                send("To%d0%s" % (i, s), mine, tp("o", 0, i), zdev[s])

        for s in SIGN:
            along(s)

        @step("fTP%d" % i)
        def _():
            wait("Th%d" % i)
            for s in SIGN:
                send("Tp%d0%s" % (i, s), tp("p", 0, i), tp("p", 0, i), zdev[s])

    def token_hop(r, i, h, s, d):
        @step("fT%s%d%d%s" % (r, i, h, s))
        def _():
            wait("T%s%d%d%s" % (r, i, h - 1, s))
            if h < 3 + is_long(i, s):
                src = tp(r, -d * h, i)
                send("T%s%d%d%s" % (r, i, h, s), src, src, zdev[s])

    for i in range(2):
        token_start(i)
        for r in "op":
            for s, d in SIGN.items():
                for h in range(1, 4 + is_long(i, s)):
                    token_hop(r, i, h, s, d)

    def as_rows(parts):
        lane = lax.broadcasted_iota(jnp.int32, (rows, 128), 1)
        tile = jnp.zeros((rows, 128), F32)
        for i, p in enumerate(parts):
            tile = jnp.where(lane == i, p, tile)
        return jnp.transpose(tile)[:8, :]

    def as_columns(parts):
        pad = jnp.zeros((128 - len(parts), rows), F32)
        return jnp.transpose(jnp.concatenate(list(parts) + [pad], axis=0))

    def stat_send(which, name, s):
        send(name, st_ring.at[which, z], st_ring.at[which, z], zdev[s])

    def stat_hop(which, p, h, s, d):
        @step("%sS%d%s" % ("fb"[which], h, s))
        def _():
            wait("%st%d%s" % (p, h - 1, s))
            if h < 3 or (h == 3 and d == 1):
                src = st_ring.at[which, ring(z, -d * h, 8)]
                send("%st%d%s" % (p, h, s), src, src, zdev[s])

    for h in range(1, 5):
        for s, d in SIGN.items():
            if h < 4 or d == 1:
                stat_hop(0, "S", h, s, d)
                stat_hop(1, "R", h, s, d)

    @step("iSt")
    def _():
        loads[0].wait()
        own = own_tok[...].astype(F32)
        mean = jnp.mean(own, axis=-1, keepdims=True)
        dev = own - mean
        st_own[0] = as_rows((mean, jnp.sum(dev * dev, axis=-1, keepdims=True)))
        send("Sth", st_own.at[0], st_peer.at[0], yhdev)

    @step("fSt")
    def _():
        wait("Sth")
        a, b = st_own[0], st_peer[0]
        gap = a[0:1] - b[0:1]
        st_ring[0, z] = jnp.concatenate(
            [
                0.5 * (a[0:1] + b[0:1]),
                a[1:2] + b[1:2] + (0.5 * width) * gap * gap,
                jnp.zeros((6, rows), F32),
            ],
            axis=0,
        )
        for s in SIGN:
            stat_send(0, "St0" + s, s)

    @step("stat")
    def _():
        got = st_ring[0]
        means = got[:, 0:1, :]
        mean = jnp.mean(means, axis=0)
        gap = means - mean[None]
        sq = jnp.sum(got[:, 1:2, :], axis=0) + (2.0 * width) * jnp.sum(gap * gap, axis=0)
        cols[0] = as_columns((mean, lax.rsqrt(sq / (16.0 * width) + EPS)))
        normed[:, rows:, :] = jnp.ones_like(normed[:, rows:, :])
        acc[...] = jnp.zeros_like(acc)

    def norm_block(r, zd):
        @step("n%s%d" % (r, zd))
        def _():
            j = feature(r, zd)
            unit = (tfull[j].astype(F32) - cols[0, :, 0:1]) * cols[0, :, 1:2]
            unit = unit.astype(BF16)
            lanes = pl.ds(pl.multiple_of((j % 2) * width, 128), width)
            normed[j // 2, :rows, lanes] = unit
            normt[j] = jnp.transpose(unit)

    far = ring(z, 4, 8) // 2
    same_x, same_y = far // 2 == lax.rem(x, 2), lax.rem(far, 2) == y

    def pick(*four):
        a, b, c_, d_ = [ring(x, xd, 4) * 2 + ys[yd] for xd, yd in four]
        return jnp.where(same_y, jnp.where(same_x, a, b), jnp.where(same_x, c_, d_))

    def product(name, k, *chips):
        @step(name)
        def _():
            for chip_name in chips:
                wait(*arrivals[chip_name])
                if chip_name == (0, "y"):
                    loads[1].wait()
            acc[...] += mm(normed[k], wfull[k], ((1,), (0,)))

    arrivals = {
        (0, "y"): ("S0y",),
        (0, "n"): ("SBy", "SAy"),
        (2, "y"): ("SAq+", "SAq-", "SBq+", "SBq-"),
        (2, "n"): ("SAyq+", "SAyq-", "SBoq+", "SBoq-"),
    }
    for s, d in SIGN.items():
        arrivals[-d, "y"] = ("SA+" + s, "SA-" + s, "SB" + s)
        arrivals[-d, "n"] = ("SAy+" + s, "SAy-" + s, "SBo" + s)
    y0, y1, y9, y2 = (0, "y"), (1, "y"), (-1, "y"), (2, "y")
    n0, n1, n9, n2 = (0, "n"), (1, "n"), (-1, "n"), (2, "n")
    product("m0", pick(y1, y0, y0, y0), y0, y1)
    product("m1", pick(y9, y2, y1, y1), y9, y2)
    product("m2", pick(n0, n0, y9, y9), n0)
    product("m3", pick(n1, n1, y2, y2), n1)
    product("m4", pick(n9, n9, n1, n0), n9)
    product("m5", pick(y0, y1, n0, n1))
    product("m6", pick(y2, y9, n9, n9))
    product("m7", pick(n2, n2, n2, n2), n2)

    def head(h):
        @step("att%d" % h)
        def _():
            if h == 0:
                loads[2].wait()
            base = 3 * h * HD
            at = [slice(base + i * HD, base + (i + 1) * HD) for i in range(3)]
            qkv = [acc[:rows, a].astype(BF16) for a in at]
            mine = slice(h * HD, (h + 1) * HD)
            out, dq, dk, dv = one_head(*qkv, og_ref[:, mine])
            att_ref[:, mine] = out.astype(BF16)
            for a, g in zip(at, (dq, dk, dv)):
                dqkv[:, a] = g.astype(BF16)
            if h == 1:
                store(att_ref, att_hbm)

    head(0)
    head(1)

    @step("bSt")
    def _():
        d = dqkv[...].astype(F32)
        st_own[1] = as_rows(
            (
                jnp.sum(d * acc[rows : rows + 1, :], axis=-1, keepdims=True),
                jnp.sum(d * acc[:rows, :], axis=-1, keepdims=True),
            )
        )
        send("Rth", st_own.at[1], st_peer.at[1], yhdev)

    @step("bSh")
    def _():
        wait("Rth")
        st_ring[1, z] = st_own[1] + st_peer[1]
        for s in SIGN:
            stat_send(1, "Rt0" + s, s)

    @step("bstat")
    def _():
        sums = jnp.sum(st_ring[1], axis=0) * (1.0 / (16.0 * width))
        cols[1] = as_columns((sums[0:1], sums[1:2]))

    def bp(r, zd, i):
        return bk.at[feature(r, zd), pl.ds(i * hrow, hrow), :]

    def add(dst, *srcs):
        total = dst[...].astype(F32)
        for src in srcs:
            total = total + src[...].astype(F32)
        dst[...] = total.astype(BF16)

    def back(r, zd):
        @step("c%s%d" % (r, zd))
        def _():
            j = feature(r, zd)
            w = wfull[j // 2, pl.ds(pl.multiple_of((j % 2) * depth, 16), depth), :]
            bk[j] = mm(dqkv[...], w, ((1,), (1,))).astype(BF16)
            if zd == 4:
                back_send(r, 0, 0, "+", 4)
                back_send(r, 1, 0, "-", 4)

    def back_send(r, i, h, s, zd):
        dst = bin.at["op".index(r), i, "+-".index(s), h]
        send("K%s%d%d%s" % (r, i, h, s), bp(r, zd, i), dst, zdev[s])

    def got(r, i, h, s):
        return bin.at["op".index(r), i, "+-".index(s), h]

    def back_hop(r, i, h, s, d):
        @step("k%s%d%d%s" % (r, i, h, s))
        def _():
            zd = d * (4 - h)
            if h > 1 or is_long(i, s):
                wait("K%s%d%d%s" % (r, i, h - 1, s))
                add(bp(r, zd, i), got(r, i, h - 1, s))
            back_send(r, i, h, s, zd)

    for r in "op":
        for zd in (0, 1, 2, 3, 4, -1, -2, -3):
            norm_block(r, zd)
            back(r, zd)
        for i in range(2):
            for h in (1, 2, 3):
                for s, d in SIGN.items():
                    back_hop(r, i, h, s, d)

    def back_end(i):
        mine = pl.ds(i * hrow, hrow)

        @step("kp%d" % i)
        def _():
            wait("Kp%d3+" % i, "Kp%d3-" % i)
            add(bp("p", 0, i), got("p", i, 3, "+"), got("p", i, 3, "-"))
            send("Kh%d" % i, bp("p", 0, i), by.at[mine, :], yhdev)

        @step("ft%d" % i)
        def _():
            wait("Ko%d3+" % i, "Ko%d3-" % i, "Kh%d" % i)
            total = bp("o", 0, i)[...].astype(F32) + by[mine, :].astype(F32)
            for s in SIGN:
                total = total + got("o", i, 3, s)[...].astype(F32)
            mean, inv = cols[0, mine, 0:1], cols[0, mine, 1:2]
            unit = (tp("o", 0, i)[...].astype(F32) - mean) * inv
            gt_ref[mine, :] = inv * (total - cols[1, mine, 0:1] - unit * cols[1, mine, 1:2])
            store(gt_ref.at[mine, :], gt_hbm.at[mine, :])

    back_end(0)
    back_end(1)

    def chip(xd, yd):
        return ring(x, xd, 4) * 2 + ys[yd]

    def gp(xd, yd, rng, lanes=slice(None)):
        return gown.at[chip(xd, yd), pl.ds(*rng), lanes]

    XS = (0, 1, -1, 2)
    TOWARD = {1: "+", -1: "-"}

    def part_name(h):
        return "" if h is None else str(h)

    def grad(xd, yd, h=None):
        lanes = slice(None) if h is None else pl.ds(h * 3 * HD, 3 * HD)
        name = "%d%s%s" % (xd, yd, part_name(h))
        yi = "yn".index(yd)

        def block(ref):
            return ref.at[chip(xd, yd), :, lanes]

        @step("g" + name)
        def _():
            out = block(gout)
            out[...] = mm(normt[2 * chip(xd, yd) + 1 - c], dqkv[:, lanes], ((1,), (0,))).astype(BF16)
            send("G" + name, out, block(gin), sib)

        @step("o" + name)
        def _():
            mine = mm(normt[2 * chip(xd, yd) + c], dqkv[:, lanes], ((1,), (0,)))
            block(gown)[...] = mine.astype(BF16)

        @step("j" + name)
        def _():
            wait("G" + name)
            add(block(gown), block(gin))
            if yd == "n":
                dst = gya.at[XS.index(xd), :, lanes]
                send("Y%d%s" % (xd, part_name(h)), gp(xd, "n", part["A"], lanes), dst, ydev)
            if xd == 2:
                for s in SIGN:
                    dst = gbq[s].at[yi, :, lanes]
                    send("BQ" + yd + s + part_name(h), gp(2, yd, part["B" + s], lanes), dst, xdev[s])
            elif xd != 0:
                s = TOWARD[xd]
                p = OTHER[s]
                send("BF" + yd + s, gp(xd, yd, part["B" + p]), gbf[p].at[yi], xdev[s])

    def sum_y(xd, h=None):
        lanes = slice(None) if h is None else pl.ds(h * 3 * HD, 3 * HD)
        name = "%d%s" % (xd, part_name(h))

        @step("ya" + name)
        def _():
            wait("Y" + name)
            add(gp(xd, "y", part["A"], lanes), gya.at[XS.index(xd), :, lanes])
            if xd == 2:
                for s in SIGN:
                    dst = gaq[s].at[:, lanes]
                    send("AQ" + s + part_name(h), gp(2, "y", part["A" + s], lanes), dst, xdev[s])
            elif xd != 0:
                s = TOWARD[xd]
                p = OTHER[s]
                send("AF" + s, gp(xd, "y", part["A" + p]), gaf[p], xdev[s])

    def sum_x(s, d):
        def along(yd):
            yi = "yn".index(yd)

            @step("bh" + yd + s)
            def _():
                wait("BQ" + yd + s + "0", "BQ" + yd + s + "1")
                add(gp(d, yd, part["B" + s]), gbq[s].at[yi])
                send("BD" + yd + s, gp(d, yd, part["B" + s]), gbd[s].at[yi], xdev[s])

        along("y")
        along("n")

        @step("ah" + s)
        def _():
            wait("AQ" + s + "0", "AQ" + s + "1")
            add(gp(d, "y", part["A" + s]), gaq[s])
            send("AD" + s, gp(d, "y", part["A" + s]), gad[s], xdev[s])

        @step("bn" + s)
        def _():
            wait("BDn" + s, "BFn" + OTHER[s])
            add(gp(0, "n", part["B" + s]), gbd[s].at[1], gbf[s].at[1])
            send("Yb" + s, gp(0, "n", part["B" + s]), gyb[s], ydev)

        def finish(rng, *terms):
            total = gp(0, "y", rng)[...].astype(F32)
            for t in terms:
                total = total + t[...].astype(F32)
            mine = pl.ds(*rng)
            gw_ref[mine, :] = total.astype(BF16)
            store(gw_ref.at[mine, :], gw_hbm.at[mine, :])

        @step("fgA" + s)
        def _():
            wait("AD" + s, "AF" + OTHER[s])
            finish(part["A" + s], gad[s], gaf[s])

        @step("fgB" + s)
        def _():
            wait("BDy" + s, "BFy" + OTHER[s], "Yb" + s)
            finish(part["B" + s], gbd[s].at[0], gbf[s].at[0], gyb[s])

    for xd in XS:
        for h in (0, 1) if xd == 2 else (None,):
            grad(xd, "y", h)
            grad(xd, "n", h)
            sum_y(xd, h)
    for s, d in SIGN.items():
        sum_x(s, d)

    for cp in loads:
        cp.start()
    barrier = pltpu.get_barrier_semaphore()
    everyone = [sib, ydev, xdev["+"], xdev["-"], zdev["+"], zdev["-"], yhdev]
    for dev in everyone:
        pl.semaphore_signal(barrier, inc=1, device_id=dev, device_id_type=MESH)
    pl.semaphore_wait(barrier, len(everyone))

    todo = list(steps.values())
    assert sorted(ORDER) == list(range(len(todo)))
    for n in ORDER:
        todo[n]()
    assert len(copies) == COPIES
    for cp in copies.values():
        cp.wait_send()
    for cp in stores:
        cp.wait()


COPIES = 166


def hand_over(*refs):
    src, dst, held, sem = refs[:3], refs[3:6], refs[6:9], refs[9]
    order = (2, 1, 0)
    loads = [pltpu.make_async_copy(src[i], held[i], sem.at[0, i]) for i in order]
    stores = [pltpu.make_async_copy(held[i], dst[i], sem.at[1, i]) for i in order]
    for cp in loads:
        cp.start()
    for load, cp in zip(loads, stores):
        load.wait()
        cp.start()
    for cp in stores:
        cp.wait()


def per_device(tokens, w_qkv, out_grad):
    rows, width = tokens.shape
    depth, wide = w_qkv.shape
    part = split_rows(depth)
    vmem = pltpu.VMEM

    def count(name):
        return part[name][1]

    a_part = {s: vmem((count("A" + s), wide), BF16) for s in SIGN}
    b_part = {s: vmem((count("B" + s), wide), BF16) for s in SIGN}
    b_pair = {s: vmem((2, count("B" + s), wide), BF16) for s in SIGN}
    scratch = [
        vmem(out_grad.shape, BF16),
        vmem(out_grad.shape, BF16),
        vmem(tokens.shape, F32),
        vmem(w_qkv.shape, BF16),
        pltpu.SemaphoreType.DMA((3,)),
        pltpu.SemaphoreType.DMA((7,)),
        vmem((8, 2 * depth, wide), BF16),
        vmem((16, rows, width), BF16),
        vmem((8, rows + 16, 2 * width), BF16),
        vmem((16, width, rows), BF16),
        vmem((rows + 16, wide), F32),
        vmem((rows, wide), BF16),
        vmem((2, rows, 128), F32),
        vmem((8, depth, wide), BF16),
        vmem((8, depth, wide), BF16),
        vmem((8, depth, wide), BF16),
        vmem((4, count("A"), wide), BF16),
        a_part, a_part, a_part, b_pair, b_pair, b_pair, b_part,
        vmem((16, rows, width), BF16),
        vmem((2, 2, 2, 4, rows // 2, width), BF16),
        vmem((rows, width), BF16),
        vmem((2, 8, rows), F32),
        vmem((2, 8, rows), F32),
        vmem((2, 8, 8, rows), F32),
        pltpu.SemaphoreType.DMA((COPIES,)),
        pltpu.SemaphoreType.DMA((COPIES,)),
    ]
    anywhere = pl.BlockSpec(memory_space=pl.ANY)
    results = pl.pallas_call(
        kernel,
        out_shape=(
            jax.ShapeDtypeStruct(out_grad.shape, BF16),
            jax.ShapeDtypeStruct(tokens.shape, F32),
            jax.ShapeDtypeStruct(w_qkv.shape, BF16),
        ),
        in_specs=[anywhere] * 3,
        out_specs=(anywhere,) * 3,
        scratch_shapes=scratch,
        compiler_params=pltpu.CompilerParams(
            collective_id=0, has_side_effects=True, vmem_limit_bytes=62 * 1024 * 1024
        ),
    )(tokens, w_qkv, out_grad)
    return pl.pallas_call(
        hand_over,
        out_shape=[jax.ShapeDtypeStruct(r.shape, r.dtype) for r in results],
        in_specs=[pl.BlockSpec(memory_space=pltpu.HBM)] * 3,
        out_specs=[pl.BlockSpec(memory_space=pltpu.HBM)] * 3,
        scratch_shapes=[vmem(r.shape, r.dtype) for r in results]
        + [pltpu.SemaphoreType.DMA((2, 3))],
    )(*results)


def solution(mesh):
    placed = (P("dp", "mp"), P("dp", "mp"), P("dp", "mp"))
    return jax.shard_map(
        per_device, mesh=mesh, in_specs=placed, out_specs=placed, check_vma=False
    )
```
